512 devices in a mesh: prow: 16 (over z), pcol: 32 (over y, x, core).
Axes of the slice: x: 4, y: 4, z: 16, core: 2. Of those that a mesh axis runs over, the one named last changes fastest.
Arguments:
- matrix: float32 [12288, 24576], P('prow', 'pcol'), may hold values from -6 to 6
- panel: float32 [12288, 512], P('prow', 'pcol'), may hold values from -0.25 to 0.25
- l_inverse: float32 [512, 512], replicated, as said below
- touched: int32 [1024], replicated, may hold values from 0 to 12287, as said below
- anchor: int32 [1024], replicated, may hold values from 0 to 12287, as said below
Outputs:
- updated: float32 [12288, 24576], P('prow', 'pcol')
The draws below stay inside these ranges and needn't reach their ends.
Inputs may be any that keep to these rules, and one draw needn't show every extreme that they name: touched[k] = k for k below 512; its last 512 entries are the pivot rows of the panel's columns, each at least its column's index; equal entries of touched have equal entries of anchor. anchor is the row ordering of the panel's interchanges, applied in turn, read at the positions in touched: it permutes the set of touched positions. l_inverse is unit lower triangular.
All inputs are finite; a program needn't handle non-finite values.
Results may differ from the reference program's by a relative error of at most 0.000057.
Values sent between devices are 32-bit elements; how exact they have to be, the bound alone decides.
A program may use at most 64 MiB of HBM per device.

```python
import math
import jax
import jax.numpy as jnp
from jax import lax

NB = 512
ROWS = 12288
COLS = 24576


def draw_l_inverse(key, part):
    key = jax.random.fold_in(key, 5)
    entries = jax.random.normal(key, (NB, NB), jnp.float32)
    strict_lower = jnp.tril(entries / math.sqrt(NB), -1)
    return strict_lower + jnp.eye(NB, dtype=jnp.float32)


def interchange_table(key):
    pivot_key = jax.random.fold_in(key, 7)
    diagonal_idx = jnp.arange(NB, dtype=jnp.int32)
    offsets = jax.random.randint(pivot_key, (NB,), 0, ROWS - diagonal_idx, dtype=jnp.int32)
    offsets = offsets.at[0].set(0)
    offsets = offsets.at[NB - 1].set(ROWS - NB)
    pivot_rows = diagonal_idx + offsets

    def apply_swap(position, ordering):
        target = pivot_rows[position]
        here_val = ordering[position]
        there_val = ordering[target]
        return ordering.at[position].set(there_val).at[target].set(here_val)
    ordering = lax.fori_loop(0, NB, apply_swap, jnp.arange(ROWS, dtype=jnp.int32))
    positions = jnp.concatenate([diagonal_idx, pivot_rows])
    return (positions, ordering[positions])


def draw_touched(key, part):
    positions, sources = interchange_table(key)
    return positions


def draw_anchor(key, part):
    positions, sources = interchange_table(key)
    return sources


def shard_levels(key, dims, shards, smallest, high):
    level, own = 1.0, jax.random.fold_in(key, 6)
    for dim, parts in shards:
        heights = jnp.exp(jax.random.uniform(jax.random.fold_in(own, dim), (parts,), jnp.float32, smallest / len(shards), high / len(shards)))
        level = level * jnp.repeat(heights, dims[dim] // parts).reshape([-1 if axis == dim else 1 for axis in range(len(dims))])
    return level


def centred(stream_key, extent, spread, reach, pieces=(), kind=jnp.bfloat16):
    values = jax.random.normal(stream_key, extent, jnp.float32) * spread
    if len(pieces) > 0:
        values = shard_levels(stream_key, extent, pieces, -0.22, 0.18) * values
    return jnp.clip(values, min=-reach, max=reach).astype(kind)


def setup_inputs(seed: int = 0) -> dict:
    key_list = jax.random.split(jax.random.key(seed), 6)
    return {
        "matrix": centred(key_list[0], (ROWS, COLS), 1.0, 6.0, ((0, 16), (1, 32)), jnp.float32),
        "panel": centred(key_list[1], (ROWS, NB), NB ** -0.5, 0.25, ((0, 16), (1, 32)), jnp.float32),
        "l_inverse": draw_l_inverse(jax.random.fold_in(key_list[5], 71), 0),
        "touched": draw_touched(jax.random.fold_in(key_list[5], 71), 0),
        "anchor": draw_anchor(jax.random.fold_in(key_list[5], 71), 0),
    }


def reference(matrix, panel, l_inverse, touched, anchor):
    ordering = jnp.arange(matrix.shape[0], dtype=jnp.int32).at[touched].set(anchor)
    permuted = matrix[ordering]
    upper_rows = jnp.dot(l_inverse, permuted[:NB], precision=lax.Precision.HIGHEST, preferred_element_type=jnp.float32)
    return permuted - jnp.dot(panel, upper_rows, precision=lax.Precision.HIGHEST, preferred_element_type=jnp.float32)
```

```python
import functools

import jax
import jax.numpy as jnp
from jax import lax
from jax.experimental import pallas as pl
from jax.experimental.pallas import tpu as pltpu
from jax.sharding import PartitionSpec as P

MESH = pl.DeviceIdType.MESH
NZ = 16
CH = 32
HALF = 16
NSTEP = 10
NB = NZ * CH
F32, BF16 = jnp.float32, jnp.bfloat16


def reach(j):
    return (j + 1) // 2 + 2


def split(x):
    hi = x.astype(BF16)
    return hi, (x - hi.astype(F32)).astype(BF16)


def dot(a, b, ca=1):
    return lax.dot_general(a, b, (((ca,), (0,)), ((), ())), preferred_element_type=F32)


def kernel(
    shape, qsrc, ssrc, inv_ref, tgt_ref, mat, pan, linv, out,
    contrib, left1, right1, left2, right2, q, t, pall, lhi, llo, whi, wlo, hot,
    p_send, p_recv, s_send, s_recv, pan_send, pan_recv,
):
    ny, nx, nc = shape
    rows, cols = mat.shape
    z = lax.axis_index("prow")
    w = lax.axis_index("pcol")
    core, x, y = w % nc, (w // nc) % nx, w // (nc * nx)
    off = z * rows
    up, down = (z + 1) % NZ, (z + NZ - 1) % NZ
    dist = (z, (NZ - z) % NZ)
    nxt = ({"prow": up}, {"prow": down})

    def pcol(yy, xx, cc):
        return {"pcol": (yy * nx + xx) * nc + cc}

    xpart = [pcol(y, (x + d) % nx, core) for d in range(1, nx)]
    ypart = [pcol((y + d) % ny, x, core) for d in range(1, ny)]
    cpart = [pcol(y, x, 1 - core)] if nc == 2 else []
    partners = list(nxt) + xpart + ypart + cpart

    t[...] = jnp.zeros_like(t)

    barrier = pltpu.get_barrier_semaphore()
    for dev in partners:
        pl.semaphore_signal(barrier, inc=1, device_id=dev, device_id_type=MESH)
    pl.semaphore_wait(barrier, len(partners))

    def remote(src, dst, ss, rs, dev):
        return pltpu.make_async_remote_copy(
            src_ref=src, dst_ref=dst, send_sem=ss, recv_sem=rs, device_id=dev, device_id_type=MESH
        )

    mine = y * nx + x

    def pan_x(i):
        return remote(pan, pall.at[mine, core], pan_send.at[i], pan_recv.at[i], xpart[i])

    def pan_y(i):
        rowset = pall.at[pl.ds(y * nx, nx), core]
        return remote(rowset, rowset, pan_send.at[nx - 1 + i], pan_recv.at[nx - 1 + i], ypart[i])

    def pan_c():
        k = nx + ny - 2
        return remote(pall.at[:, core], pall.at[:, core], pan_send.at[k], pan_recv.at[k], cpart[0])

    def home(d, k):
        if k == 0:
            src = contrib.at[pl.ds(112, HALF)] if d == 0 else contrib.at[pl.ds(0, HALF)]
            dst = (left1, right1)[d]
        else:
            src = contrib.at[pl.ds(80, CH)] if d == 0 else contrib.at[pl.ds(16, CH)]
            dst = (left2, right2)[d]
        i = 2 * k + d
        return remote(src, dst, p_send.at[i], p_recv.at[i], nxt[d])

    def gather(d, k):
        src, dst = ((5 - k) % NZ, (4 - k) % NZ) if d == 0 else (3 + k, 4 + k)
        part = pl.ds(0, CH) if k < 8 else pl.ds(HALF * d, HALF)
        i = 4 + 2 * (k - 1) + d
        return remote(q.at[src, part], q.at[dst, part], p_send.at[i], p_recv.at[i], nxt[d])

    def take_rows(first, count):
        def one(i, _):
            r = first + i
            li = qsrc[80 + r] - off
            row = mat[pl.ds(jnp.clip(li, 0, rows - 1), 1), :]
            contrib[pl.ds(r, 1), :] = jnp.where((li >= 0) & (li < rows), row, 0.0)
            return 0

        lax.fori_loop(0, count, one, 0, unroll=4)

    def piece(d, j):
        return j if d == 0 else 31 - j

    def scatter(d, j):
        c = piece(d, j)
        return remote(t.at[c], t.at[c], s_send.at[d, j], s_recv.at[d, j], nxt[d])

    def pieces(b):
        first = 15 - 2 * b - jnp.minimum(b, 2)
        return [(first - u, (b >= 0) & (b <= 6) & ((u < 2) | (b < 2))) for u in range(3)]

    def fill(b):
        if b > 6:
            return
        first, count = 15 - 2 * b - min(b, 2), 3 if b < 2 else 2

        @pl.when(z == 0)
        def _():
            for d in (0, 1):
                base = HALF * (first - count + 1 if d == 0 else 31 - first)

                def one(i, _):
                    r = base + i
                    row = mat[pl.ds(jnp.clip(ssrc[r], 0, rows - 1), 1), :]
                    t[r // HALF, pl.ds(r % HALF, 1), :] = row
                    return 0

                lax.fori_loop(0, HALF * count, one, 0, unroll=4)

    def pass_on(step):
        for d in (0, 1):
            for j, valid in pieces(step - dist[d]):
                j = jnp.clip(j, 0, 15)

                @pl.when(valid & (dist[d] >= 1) & (dist[d] <= reach(j)))
                def _():
                    scatter(d, j).wait_recv()

                if step < NSTEP:

                    @pl.when(valid & (dist[d] < reach(j)))
                    def _():
                        scatter(d, j).start()

    def order():
        kk = lax.broadcasted_iota(jnp.int32, (NB, NB), 0)
        perm = (kk == inv_ref[...]).astype(F32).astype(BF16)
        hi, lo = split(linv[...])
        lhi[...] = dot(hi, perm).astype(BF16)
        llo[...] = dot(lo, perm).astype(BF16)

    def base():
        for r in range(0, rows, 256):
            qq = lax.broadcasted_iota(jnp.int32, (256, NB), 0) + r
            hit = (qq + off == tgt_ref[...]).astype(F32)
            hot[pl.ds(r, 256), :] = hit.astype(BF16)
            gone = jnp.max(hit, axis=1, keepdims=True) > 0.0
            top = (lax.broadcasted_iota(jnp.int32, (256, 1), 0) + r < NB) & (z == 0)
            out[pl.ds(r, 256), :] = jnp.where(gone | top, 0.0, mat[pl.ds(r, 256), :])

    def weights(r):
        a = pall[...].reshape(NB, rows)[:, r:r + 256]
        ahi, alo = split(a)
        acc = dot(ahi, lhi[...], 0) + dot(ahi, llo[...], 0) + dot(alo, lhi[...], 0)
        qq = lax.broadcasted_iota(jnp.int32, (256, NB), 0) + r
        own = (qq == inv_ref[...]) & (z == 0)
        acc = acc - own.astype(F32)
        hi, lo = split(acc)
        whi[pl.ds(r, 256), :] = hi
        wlo[pl.ds(r, 256), :] = lo

    def update(k, c):
        qhi, qlo = split(q[k // CH:k // CH + 8, :, c:c + 256].reshape(256, 256))
        a, b = whi[:, k:k + 256], wlo[:, k:k + 256]
        out[:, c:c + 256] -= dot(a, qhi) + dot(a, qlo) + dot(b, qhi)

    def moved(c):
        thi, tlo = split(t[:, :, c:c + 256].reshape(NB, 256))
        out[:, c:c + 256] += dot(hot[...], thi) + dot(hot[...], tlo)

    stripes = list(range(0, cols, 256))

    for i in range(nx - 1):
        pan_x(i).start()
    take_rows(0, HALF)
    take_rows(112, HALF)
    home(0, 0).start()
    home(1, 0).start()
    fill(0)
    pass_on(0)
    take_rows(16, CH)
    take_rows(80, CH)
    pall[mine, core] = pan[...]

    home(0, 0).wait_recv()
    contrib[pl.ds(80, HALF), :] += left1[...]
    home(0, 1).start()
    home(1, 0).wait_recv()
    contrib[pl.ds(32, HALF), :] += right1[...]
    home(1, 1).start()
    fill(1)
    pass_on(1)
    take_rows(48, CH)
    fill(2)
    for i in range(nx - 1):
        pan_x(i).wait_recv()
    for i in range(ny - 1):
        pan_y(i).start()

    home(0, 1).wait_recv()
    home(1, 1).wait_recv()
    q[4] = contrib[pl.ds(48, CH), :] + left2[...] + right2[...]
    for k in range(1, 9):
        if k > 1:
            gather(0, k - 1).wait_recv()
        gather(0, k).start()
        if k > 1:
            gather(1, k - 1).wait_recv()
        gather(1, k).start()
        pass_on(1 + k)
        fill(2 + k)
        if k == 1:
            order()
        if k == 2:
            base()
        if k == 3:
            for i in range(ny - 1):
                pan_y(i).wait_recv()
            if cpart:
                pan_c().start()
        if k == 4:
            if cpart:
                pan_c().wait_recv()
            for r in range(0, rows, 256):
                weights(r)
        if k >= 5 and k - 5 < len(stripes):
            update(0, stripes[k - 5])
    gather(0, 8).wait_recv()
    gather(1, 8).wait_recv()
    pass_on(NSTEP)
    for c in stripes:
        moved(c)
        update(256, c)

    for d in (0, 1):
        home(d, 0).wait_send()
        home(d, 1).wait_send()
        for k in range(1, 9):
            gather(d, k).wait_send()

        def sent(j, _):
            @pl.when(dist[d] < reach(j))
            def _():
                scatter(d, j).wait_send()

            return 0

        lax.fori_loop(0, 16, sent, 0)
    for i in range(nx - 1):
        pan_x(i).wait_send()
    for i in range(ny - 1):
        pan_y(i).wait_send()
    if cpart:
        pan_c().wait_send()


def plan(touched, anchor, rows, z):
    idx = jnp.arange(NB, dtype=jnp.int32)
    src, owner = anchor[:NB], anchor[:NB] // rows
    tgt, top = touched[NB:], anchor[NB:]
    dest = tgt // rows
    again = jnp.any((tgt[None, :] == tgt[:, None]) & (idx[None, :] < idx[:, None]), axis=1)
    tgt = jnp.where(again | (tgt < NB), -1, tgt)

    def rank(group):
        key = group * NB + idx
        return jnp.sum((key[None, :] < key[:, None]).astype(jnp.int32), axis=1)

    def place(pos, values):
        return jnp.sum(jnp.where(pos[:, None] == idx[None, :], values[:, None], 0), axis=0)

    r, s = rank(owner), rank(dest)
    away = (owner - r // CH + 8) % NZ - 8
    late = r % CH >= HALF
    fits = (jnp.abs(away) <= 1) | ((away == -2) & ~late) | ((away == 2) & late)
    hops = jnp.where(s < NB // 2, dest, NZ - dest)
    near = jnp.where(s < NB // 2, s, NB - 1 - s) // HALF
    fits &= (tgt < rows) | (hops <= reach(near))
    here = (r - CH * z + 4 * CH) % NB
    return jnp.all(fits), place(here, src), place(s, top), place(here, idx), place(s, tgt)


def plain(matrix, panel_t, l_inverse, touched, anchor):
    rows = matrix.shape[0]
    offset = lax.axis_index("prow") * rows
    local = anchor - offset
    owned = (local >= 0) & (local < rows)
    picked = jnp.where(owned[:, None], matrix[jnp.clip(local, 0, rows - 1)], 0.0)

    def ring(axis, init):
        n = lax.axis_size(axis)
        pairs = [(i, (i + 1) % n) for i in range(n)]
        return n, lambda v: lax.ppermute(v, axis, pairs), init

    n, shift, _ = ring("prow", None)

    def add(_, carry):
        part, total = carry
        part = shift(part)
        return part, total + part

    _, moved = lax.fori_loop(0, n - 1, add, (picked, picked))
    m, shift_p, _ = ring("pcol", None)
    me = lax.axis_index("pcol")
    wide = jnp.zeros((m,) + panel_t.shape, panel_t.dtype).at[me].set(panel_t)

    def put(i, carry):
        part, whole = carry
        part = shift_p(part)
        return part, lax.dynamic_update_index_in_dim(whole, part, (me - 1 - i) % m, 0)

    _, wide = lax.fori_loop(0, m - 1, put, (panel_t, wide))
    high = functools.partial(jnp.dot, precision=lax.Precision.HIGHEST, preferred_element_type=F32)
    upper = high(l_inverse, moved[:NB])
    target = touched - offset
    target = jnp.where((target >= 0) & (target < rows), target, rows)
    permuted = matrix.at[target].set(moved, mode="drop")
    return permuted - high(wide.reshape(NB, rows).T, upper)


def fast(shape, matrix, panel_t, l_inverse, qsrc, ssrc, inv, tgt):
    rows, cols = matrix.shape
    ny, nx, nc = shape
    vmem, smem = pl.BlockSpec(memory_space=pltpu.VMEM), pl.BlockSpec(memory_space=pltpu.SMEM)
    npan = max(nx + ny - 1, 1)
    dma = pltpu.SemaphoreType.DMA
    return pl.pallas_call(
        functools.partial(kernel, shape),
        out_shape=jax.ShapeDtypeStruct((rows, cols), F32),
        in_specs=[smem, smem] + [vmem] * 5,
        out_specs=vmem,
        scratch_shapes=[
            pltpu.VMEM((128, cols), F32),
            pltpu.VMEM((HALF, cols), F32),
            pltpu.VMEM((HALF, cols), F32),
            pltpu.VMEM((CH, cols), F32),
            pltpu.VMEM((CH, cols), F32),
            pltpu.VMEM((NZ, CH, cols), F32),
            pltpu.VMEM((32, HALF, cols), F32),
            pltpu.VMEM((ny * nx, nc, panel_t.shape[0], rows), F32),
            pltpu.VMEM((NB, NB), BF16),
            pltpu.VMEM((NB, NB), BF16),
            pltpu.VMEM((rows, NB), BF16),
            pltpu.VMEM((rows, NB), BF16),
            pltpu.VMEM((rows, NB), BF16),
            dma((20,)), dma((20,)), dma((2, 16)), dma((2, 16)), dma((npan,)), dma((npan,)),
        ],
        compiler_params=pltpu.CompilerParams(
            collective_id=0, has_side_effects=True, vmem_limit_bytes=48 * 2**20
        ),
    )(qsrc, ssrc, inv.reshape(1, NB), tgt.reshape(1, NB), matrix, panel_t, l_inverse)


def body(shape, matrix, panel, l_inverse, touched, anchor):
    z = lax.axis_index("prow")
    fits, qsrc, ssrc, inv, tgt = plan(touched, anchor, matrix.shape[0], z)
    panel_t = panel.T
    return lax.cond(
        fits,
        lambda: fast(shape, matrix, panel_t, l_inverse, qsrc, ssrc, inv, tgt),
        lambda: plain(matrix, panel_t, l_inverse, touched, anchor),
    )


def solution(mesh):
    n = mesh.shape["pcol"]
    shape = (4, 4, 2) if n == 32 else (1, n, 1)
    in_specs = (P("prow", "pcol"), P("prow", "pcol"), P(), P(), P())
    return jax.shard_map(
        functools.partial(body, shape), mesh=mesh, in_specs=in_specs, out_specs=P("prow", "pcol"), check_vma=False
    )
```

```python
import functools

import jax
import jax.numpy as jnp
from jax import lax
from jax.experimental import pallas as pl
from jax.experimental.pallas import tpu as pltpu
from jax.sharding import PartitionSpec as P

MESH = pl.DeviceIdType.MESH
NZ = 16
CH = 32
HALF = 16
WIN = 256
NB = NZ * CH
F32, BF16 = jnp.float32, jnp.bfloat16


def reach(j):
    return (j + 1) // 2 + 2


UPWARDS = [(8, 7)] * NZ
KSTEP = max(max(a, NZ - 1 - a) for p in UPWARDS for a in p)
BLOCKS = [2] * 8


def window(z):
    return jnp.clip(2 * z - 7, 0, 16)


def split(x):
    hi = x.astype(BF16)
    return hi, (x - hi.astype(F32)).astype(BF16)


def dot(a, b, ca=1):
    return lax.dot_general(a, b, (((ca,), (0,)), ((), ())), preferred_element_type=F32)


def kernel(
    shape, qsrc, ssrc, inv_ref, tgt_ref, mat_hbm, pan, linv_hbm, out,
    mat, linv, contrib, left1, right1, left2, right2, q, t, pall, lhi, llo, whi, wlo, hot,
    p_send, p_recv, g_send, g_recv, s_send, s_recv, pan_send, pan_recv, load,
):
    ny, nx, nc = shape
    rows, cols = mat.shape
    z = lax.axis_index("prow")
    w = lax.axis_index("pcol")
    core, x, y = w % nc, (w // nc) % nx, w // (nc * nx)
    off = z * rows
    up, down = (z + 1) % NZ, (z + NZ - 1) % NZ
    dist = (z, (NZ - z) % NZ)
    nxt = ({"prow": up}, {"prow": down})

    def pcol(yy, xx, cc):
        return {"pcol": (yy * nx + xx) * nc + cc}

    xpart = [pcol(y, (x + d) % nx, core) for d in range(1, nx)]
    ypart = [pcol((y + d) % ny, x, core) for d in range(1, ny)]
    cpart = [pcol(y, x, 1 - core)] if nc == 2 else []
    partners = list(nxt) + xpart + ypart + cpart
    mine = y * nx + x

    loads = [
        pltpu.make_async_copy(mat_hbm, mat, load.at[0]),
        pltpu.make_async_copy(linv_hbm, linv, load.at[1]),
        pltpu.make_async_copy(pan, pall.at[mine, core], load.at[2]),
    ]
    for c in loads:
        c.start()
    t[...] = jnp.zeros_like(t)

    barrier = pltpu.get_barrier_semaphore()
    for dev in partners:
        pl.semaphore_signal(barrier, inc=1, device_id=dev, device_id_type=MESH)
    pl.semaphore_wait(barrier, len(partners))

    def remote(src, dst, ss, rs, dev):
        return pltpu.make_async_remote_copy(
            src_ref=src, dst_ref=dst, send_sem=ss, recv_sem=rs, device_id=dev, device_id_type=MESH
        )

    def on(devices, act):
        if len(devices) == NZ:
            act()
            return
        starts = [i for i in sorted(devices) if (i - 1) % NZ not in devices]
        hit = None
        for i in starts:
            n = 1
            while (i + n) % NZ in devices:
                n += 1
            one = (z + NZ - i) % NZ < n
            hit = one if hit is None else hit | one
        if hit is not None:
            pl.when(hit)(act)

    def pan_x(i):
        return remote(pan, pall.at[mine, core], pan_send.at[i], pan_recv.at[i], xpart[i])

    def pan_y(i):
        rowset = pall.at[pl.ds(y * nx, nx), core]
        return remote(rowset, rowset, pan_send.at[nx - 1 + i], pan_recv.at[nx - 1 + i], ypart[i])

    def pan_c():
        k = nx + ny - 2
        return remote(pall.at[:, core], pall.at[:, core], pan_send.at[k], pan_recv.at[k], cpart[0])

    def home(d, k):
        if k == 0:
            src = contrib.at[pl.ds(112, HALF)] if d == 0 else contrib.at[pl.ds(0, HALF)]
            dst = (left1, right1)[d]
        else:
            src = contrib.at[pl.ds(80, CH)] if d == 0 else contrib.at[pl.ds(16, CH)]
            dst = (left2, right2)[d]
        i = 2 * k + d
        return remote(src, dst, p_send.at[i], p_recv.at[i], nxt[d])

    def gather(d, k, u):
        src, dst = ((5 - k) % NZ, (4 - k) % NZ) if d == 0 else (3 + k, 4 + k)
        part = pl.ds(HALF * u, HALF)
        i = (2 * (k - 1) + d) * 2 + u
        return remote(q.at[src, part], q.at[dst, part], g_send.at[i], g_recv.at[i], nxt[d])

    def senders(d, k, u):
        keep = set()
        for i in range(NZ):
            h = (i - (k - 1)) % NZ if d == 0 else (i + (k - 1)) % NZ
            far = UPWARDS[h][u] if d == 0 else NZ - 1 - UPWARDS[h][u]
            if k <= far:
                keep.add(i)
        return keep

    def ring(k):
        for u in (0, 1):
            for d in (0, 1):
                if k > 1:
                    came = {(i + (1 if d == 0 else -1)) % NZ for i in senders(d, k - 1, u)}
                    on(came, lambda: gather(d, k - 1, u).wait_recv())
                if k <= KSTEP:
                    on(senders(d, k, u), lambda: gather(d, k, u).start())

    def take_rows(first, count):
        def one(i, _):
            r = first + i
            li = qsrc[80 + r] - off
            row = mat[pl.ds(jnp.clip(li, 0, rows - 1), 1), :]
            contrib[pl.ds(r, 1), :] = jnp.where((li >= 0) & (li < rows), row, 0.0)
            return 0

        lax.fori_loop(0, count, one, 0, unroll=8)

    def piece(d, j):
        return j if d == 0 else 31 - j

    def scatter(d, j):
        c = piece(d, j)
        return remote(t.at[c], t.at[c], s_send.at[d, j], s_recv.at[d, j], nxt[d])

    nblocks = len(BLOCKS)
    first_of = [15 - sum(BLOCKS[:b]) for b in range(nblocks)]

    def fill(b):
        if b >= nblocks:
            return

        @pl.when(z == 0)
        def _():
            for d in (0, 1):
                base = HALF * (first_of[b] - BLOCKS[b] + 1 if d == 0 else 31 - first_of[b])

                def one(i, _):
                    r = base + i
                    row = mat[pl.ds(jnp.clip(ssrc[r], 0, rows - 1), 1), :]
                    t[r // HALF, pl.ds(r % HALF, 1), :] = row
                    return 0

                lax.fori_loop(0, HALF * BLOCKS[b], one, 0, unroll=8)

    def pass_on(step):
        for d in (0, 1):
            b = step - dist[d]
            first, count = jnp.int32(0), jnp.int32(0)
            for i in range(nblocks):
                first = jnp.where(b == i, first_of[i], first)
                count = jnp.where(b == i, BLOCKS[i], count)
            for u in range(max(BLOCKS)):
                j = jnp.clip(first - u, 0, 15)
                valid = u < count

                @pl.when(valid & (dist[d] >= 1) & (dist[d] <= reach(j)))
                def _():
                    scatter(d, j).wait_recv()

                @pl.when(valid & (dist[d] < reach(j)))
                def _():
                    scatter(d, j).start()

    def order():
        loads[1].wait()
        kk = lax.broadcasted_iota(jnp.int32, (NB, NB), 0)
        perm = (kk == inv_ref[...]).astype(F32).astype(BF16)
        hi, lo = split(linv[...])
        lhi[...] = dot(hi, perm).astype(BF16)
        llo[...] = dot(lo, perm).astype(BF16)

    def base():
        for r in range(0, rows, 256):
            qq = lax.broadcasted_iota(jnp.int32, (256, WIN), 0) + r
            hit = (qq + off == tgt_ref[...]).astype(F32)
            hot[pl.ds(r, 256), :] = hit.astype(BF16)
            gone = jnp.max(hit, axis=1, keepdims=True) > 0.0
            top = (lax.broadcasted_iota(jnp.int32, (256, 1), 0) + r < NB) & (z == 0)
            out[pl.ds(r, 256), :] = jnp.where(gone | top, 0.0, mat[pl.ds(r, 256), :])

    def weights(r):
        a = pall[:, :, :, r:r + 256].reshape(NB, 256)
        ahi, alo = split(a)
        acc = dot(ahi, lhi[...], 0) + dot(ahi, llo[...], 0) + dot(alo, lhi[...], 0)
        qq = lax.broadcasted_iota(jnp.int32, (256, NB), 0) + r
        own = (qq == inv_ref[...]) & (z == 0)
        acc = acc - own.astype(F32)
        hi, lo = split(acc)
        whi[pl.ds(r, 256), :] = hi
        wlo[pl.ds(r, 256), :] = lo

    def product(k, c):
        qhi, qlo = split(q[k // CH:k // CH + 8, :, c:c + 256].reshape(256, 256))
        a, b = whi[:, k:k + 256], wlo[:, k:k + 256]
        return dot(a, qhi) + dot(a, qlo) + dot(b, qhi)

    def update(c):
        out[:, c:c + 256] -= product(0, c)

    def finish(c):
        thi, tlo = split(t[pl.ds(window(z), 16), :, c:c + 256].reshape(WIN, 256))
        out[:, c:c + 256] += dot(hot[...], thi) + dot(hot[...], tlo) - product(256, c)

    stripes = list(range(0, cols, 256))
    later = {1: [order], 2: [base]}
    for i in range(3):
        later[3 + i] = [functools.partial(weights, 256 * i)]
    for i, c in enumerate(stripes):
        later[6 + i] = [functools.partial(update, c)]

    for i in range(nx - 1):
        pan_x(i).start()
    loads[0].wait()
    take_rows(0, HALF)
    take_rows(112, HALF)
    home(0, 0).start()
    home(1, 0).start()
    fill(0)
    pass_on(0)
    take_rows(16, CH)
    take_rows(80, CH)

    home(0, 0).wait_recv()
    contrib[pl.ds(80, HALF), :] += left1[...]
    home(0, 1).start()
    home(1, 0).wait_recv()
    contrib[pl.ds(32, HALF), :] += right1[...]
    home(1, 1).start()
    fill(1)
    pass_on(1)
    take_rows(48, CH)
    fill(2)
    loads[2].wait()
    for i in range(nx - 1):
        pan_x(i).wait_recv()
    for i in range(ny - 1):
        pan_y(i).start()

    home(0, 1).wait_recv()
    home(1, 1).wait_recv()
    q[4] = contrib[pl.ds(48, CH), :] + left2[...] + right2[...]
    for k in range(1, KSTEP + 1):
        ring(k)
        pass_on(1 + k)
        fill(2 + k)
        if k == 2:
            for i in range(ny - 1):
                pan_y(i).wait_recv()
            if cpart:
                pan_c().start()
        if k == 3 and cpart:
            pan_c().wait_recv()
        for f in later.pop(k, []):
            f()
    for fs in later.values():
        for f in fs:
            f()
    for step in range(KSTEP + 2, nblocks + 10):
        pass_on(step)
    ring(KSTEP + 1)
    for c in stripes:
        finish(c)

    for d in (0, 1):
        home(d, 0).wait_send()
        home(d, 1).wait_send()
        for k in range(1, KSTEP + 1):
            for u in (0, 1):
                on(senders(d, k, u), lambda: gather(d, k, u).wait_send())

        def sent(j, _):
            @pl.when(dist[d] < reach(j))
            def _():
                scatter(d, j).wait_send()

            return 0

        lax.fori_loop(0, 16, sent, 0)
    for i in range(nx - 1):
        pan_x(i).wait_send()
    for i in range(ny - 1):
        pan_y(i).wait_send()
    if cpart:
        pan_c().wait_send()


def plan(touched, anchor, rows, z):
    idx = jnp.arange(NB, dtype=jnp.int32)
    src, owner = anchor[:NB], anchor[:NB] // rows
    tgt, top = touched[NB:], anchor[NB:]
    dest = tgt // rows

    def rank(group):
        key = group * NB + idx
        return jnp.sum((key[None, :] < key[:, None]).astype(jnp.int32), axis=1)

    def place(pos, values):
        return jnp.sum(jnp.where(pos[:, None] == idx[None, :], values[:, None], 0), axis=0)

    r, s = rank(owner), rank(tgt)
    here = (r - CH * z + 4 * CH) % NB
    one = place(here, src * NB + idx)
    two = place(s, tgt * NB + jnp.clip(top, 0, NB - 1))
    goes = two // NB
    before = jnp.concatenate([jnp.full((1,), -1, jnp.int32), goes[:-1]])
    goes = jnp.where((goes < NB) | (goes == before), -1, goes)
    goes = lax.dynamic_slice_in_dim(goes, HALF * window(z), WIN)

    away = (owner - r // CH + 8) % NZ - 8
    late = r % CH >= HALF
    fits = (jnp.abs(away) <= 1) | ((away == -2) & ~late) | ((away == 2) & late)
    hops = jnp.where(s < NB // 2, dest, NZ - dest)
    near = jnp.where(s < NB // 2, s, NB - 1 - s) // HALF
    inside = s - HALF * window(dest)
    fits &= (tgt < NB) | ((inside >= 0) & (inside < WIN) & ((dest == 0) | (hops <= reach(near))))
    return jnp.all(fits), one // NB, two % NB, one % NB, goes


def plain(matrix, panel_t, l_inverse, touched, anchor):
    rows = matrix.shape[0]
    offset = lax.axis_index("prow") * rows
    local = anchor - offset
    owned = (local >= 0) & (local < rows)
    picked = jnp.where(owned[:, None], matrix[jnp.clip(local, 0, rows - 1)], 0.0)

    def ring(axis, init):
        n = lax.axis_size(axis)
        pairs = [(i, (i + 1) % n) for i in range(n)]
        return n, lambda v: lax.ppermute(v, axis, pairs), init

    n, shift, _ = ring("prow", None)

    def add(_, carry):
        part, total = carry
        part = shift(part)
        return part, total + part

    _, moved = lax.fori_loop(0, n - 1, add, (picked, picked))
    m, shift_p, _ = ring("pcol", None)
    me = lax.axis_index("pcol")
    wide = jnp.zeros((m,) + panel_t.shape, panel_t.dtype).at[me].set(panel_t)

    def put(i, carry):
        part, whole = carry
        return shift_p(part), lax.dynamic_update_index_in_dim(whole, part, (me - 1 - i) % m, 0)

    _, wide = lax.fori_loop(0, m - 1, put, (shift_p(panel_t), wide))
    high = functools.partial(jnp.dot, precision=lax.Precision.HIGHEST, preferred_element_type=F32)
    upper = high(l_inverse, moved[:NB])
    target = touched - offset
    target = jnp.where((target >= 0) & (target < rows), target, rows)
    lands = jnp.full((rows,), -1, jnp.int32).at[target].set(jnp.arange(2 * NB, dtype=jnp.int32), mode="drop")
    permuted = jnp.where((lands >= 0)[:, None], moved[jnp.clip(lands, 0, 2 * NB - 1)], matrix)
    return permuted - high(wide.reshape(NB, rows).T, upper)


def fast(shape, matrix, panel_t, l_inverse, qsrc, ssrc, inv, tgt):
    rows, cols = matrix.shape
    ny, nx, nc = shape
    vmem, smem = pl.BlockSpec(memory_space=pltpu.VMEM), pl.BlockSpec(memory_space=pltpu.SMEM)
    hbm = pl.BlockSpec(memory_space=pl.ANY)
    npan = max(nx + ny - 1, 1)
    dma = pltpu.SemaphoreType.DMA
    return pl.pallas_call(
        functools.partial(kernel, shape),
        out_shape=pltpu.VMEM((rows, cols), F32),
        in_specs=[smem, smem, vmem, vmem, hbm, hbm, hbm],
        out_specs=vmem,
        scratch_shapes=[
            pltpu.VMEM((rows, cols), F32),
            pltpu.VMEM((NB, NB), F32),
            pltpu.VMEM((128, cols), F32),
            pltpu.VMEM((HALF, cols), F32),
            pltpu.VMEM((HALF, cols), F32),
            pltpu.VMEM((CH, cols), F32),
            pltpu.VMEM((CH, cols), F32),
            pltpu.VMEM((NZ, CH, cols), F32),
            pltpu.VMEM((32, HALF, cols), F32),
            pltpu.VMEM((ny * nx, nc, panel_t.shape[0], rows), F32),
            pltpu.VMEM((NB, NB), BF16),
            pltpu.VMEM((NB, NB), BF16),
            pltpu.VMEM((rows, NB), BF16),
            pltpu.VMEM((rows, NB), BF16),
            pltpu.VMEM((rows, WIN), BF16),
            dma((4,)), dma((4,)), dma((4 * KSTEP,)), dma((4 * KSTEP,)),
            dma((2, 16)), dma((2, 16)), dma((npan,)), dma((npan,)), dma((3,)),
        ],
        compiler_params=pltpu.CompilerParams(
            collective_id=0, has_side_effects=True, vmem_limit_bytes=40 * 2**20
        ),
    )(qsrc, ssrc, inv.reshape(1, NB), tgt.reshape(1, WIN), matrix, panel_t, l_inverse)


def body(shape, matrix, panel, l_inverse, touched, anchor):
    z = lax.axis_index("prow")
    fits, qsrc, ssrc, inv, tgt = plan(touched, anchor, matrix.shape[0], z)
    panel_t = panel.T
    done = fast(shape, matrix, panel_t, l_inverse, qsrc, ssrc, inv, tgt)
    return lax.cond(fits, lambda: done, lambda: plain(matrix, panel_t, l_inverse, touched, anchor))


def solution(mesh):
    n = mesh.shape["pcol"]
    shape = (4, 4, 2) if n == 32 else (1, n, 1)
    in_specs = (P("prow", "pcol"), P("prow", "pcol"), P(), P(), P())
    return jax.shard_map(
        functools.partial(body, shape), mesh=mesh, in_specs=in_specs, out_specs=P("prow", "pcol"), check_vma=False
    )
```

```python
import functools

import jax
import jax.numpy as jnp
from jax import lax
from jax.experimental import pallas as pl
from jax.experimental.pallas import tpu as pltpu
from jax.sharding import PartitionSpec as P

MESH = pl.DeviceIdType.MESH
NZ = 16
CH = 32
HALF = 16
WIN = 256
NB = NZ * CH
BITS = 9
F32, BF16 = jnp.float32, jnp.bfloat16


def reach(j):
    return (j + 1) // 2 + 2


UPWARDS = [
    (5, 5), (7, 7), (6, 11), (11, 11), (11, 11), (10, 10), (10, 10), (9, 9),
    (7, 7), (6, 6), (6, 6), (5, 5), (4, 4), (4, 4), (4, 6), (7, 7),
]
KSTEP = max(max(a, NZ - 1 - a) for p in UPWARDS for a in p)
BLOCKS = [0, 1, 1, 1, 1, 2, 2, 2, 2, 2, 2]


def window(z):
    return jnp.clip(2 * z - 7, 0, 16)


def split(x):
    hi = x.astype(BF16)
    return hi, (x - hi.astype(F32)).astype(BF16)


def dot(a, b, ca=1):
    return lax.dot_general(a, b, (((ca,), (0,)), ((), ())), preferred_element_type=F32)


def kernel(
    shape, one_smem, two_smem, one_ref, two_ref, tgt_ref, mat_hbm, pan, linv_hbm, out, misfit,
    mat, linv, contrib, left1, right1, left2, right2, q, t, pall, lhi, llo, whi, wlo, hot,
    p_send, p_recv, g_send, g_recv, s_send, s_recv, pan_send, pan_recv, load,
):
    ny, nx, nc = shape
    rows, cols = mat.shape
    z = lax.axis_index("prow")
    w = lax.axis_index("pcol")
    core, x, y = w % nc, (w // nc) % nx, w // (nc * nx)
    off = z * rows
    up, down = (z + 1) % NZ, (z + NZ - 1) % NZ
    dist = (z, (NZ - z) % NZ)
    nxt = ({"prow": up}, {"prow": down})

    def pcol(yy, xx, cc):
        return {"pcol": (yy * nx + xx) * nc + cc}

    xpart = [pcol(y, (x + d) % nx, core) for d in range(1, nx)]
    ypart = [pcol((y + d) % ny, x, core) for d in range(1, ny)]
    cpart = [pcol(y, x, 1 - core)] if nc == 2 else []
    partners = list(nxt) + xpart + ypart + cpart
    mine = y * nx + x

    loads = [
        pltpu.make_async_copy(mat_hbm, mat, load.at[0]),
        pltpu.make_async_copy(linv_hbm, linv, load.at[1]),
        pltpu.make_async_copy(pan, pall.at[mine, core], load.at[2]),
    ]
    for c in loads:
        c.start()
    t[...] = jnp.zeros_like(t)

    barrier = pltpu.get_barrier_semaphore()
    for dev in partners:
        pl.semaphore_signal(barrier, inc=1, device_id=dev, device_id_type=MESH)
    pl.semaphore_wait(barrier, len(partners))

    def remote(src, dst, ss, rs, dev):
        return pltpu.make_async_remote_copy(
            src_ref=src, dst_ref=dst, send_sem=ss, recv_sem=rs, device_id=dev, device_id_type=MESH
        )

    def on(devices, act):
        if len(devices) == NZ:
            act()
            return
        starts = [i for i in sorted(devices) if (i - 1) % NZ not in devices]
        hit = None
        for i in starts:
            n = 1
            while (i + n) % NZ in devices:
                n += 1
            one = (z + NZ - i) % NZ < n
            hit = one if hit is None else hit | one
        if hit is not None:
            pl.when(hit)(act)

    def pan_x(i):
        return remote(pan, pall.at[mine, core], pan_send.at[i], pan_recv.at[i], xpart[i])

    def pan_y(i):
        rowset = pall.at[pl.ds(y * nx, nx), core]
        return remote(rowset, rowset, pan_send.at[nx - 1 + i], pan_recv.at[nx - 1 + i], ypart[i])

    def pan_c():
        k = nx + ny - 2
        return remote(pall.at[:, core], pall.at[:, core], pan_send.at[k], pan_recv.at[k], cpart[0])

    def home(d, k):
        if k == 0:
            src = contrib.at[pl.ds(112, HALF)] if d == 0 else contrib.at[pl.ds(0, HALF)]
            dst = (left1, right1)[d]
        else:
            src = contrib.at[pl.ds(80, CH)] if d == 0 else contrib.at[pl.ds(16, CH)]
            dst = (left2, right2)[d]
        i = 2 * k + d
        return remote(src, dst, p_send.at[i], p_recv.at[i], nxt[d])

    def gather(d, k, u):
        src, dst = ((5 - k) % NZ, (4 - k) % NZ) if d == 0 else (3 + k, 4 + k)
        part = pl.ds(HALF * u, HALF)
        i = (2 * (k - 1) + d) * 2 + u
        return remote(q.at[src, part], q.at[dst, part], g_send.at[i], g_recv.at[i], nxt[d])

    def senders(d, k, u):
        keep = set()
        for i in range(NZ):
            h = (i - (k - 1)) % NZ if d == 0 else (i + (k - 1)) % NZ
            far = UPWARDS[h][u] if d == 0 else NZ - 1 - UPWARDS[h][u]
            if k <= far:
                keep.add(i)
        return keep

    def ring(k):
        for u in (0, 1):
            for d in (0, 1):
                if k > 1:
                    came = {(i + (1 if d == 0 else -1)) % NZ for i in senders(d, k - 1, u)}
                    on(came, lambda: gather(d, k - 1, u).wait_recv())
                if k <= KSTEP:
                    on(senders(d, k, u), lambda: gather(d, k, u).start())

    def take_rows(first, count):
        def one(i, _):
            r = first + i
            li = (one_smem[80 + r] >> BITS) - off
            row = mat[pl.ds(jnp.clip(li, 0, rows - 1), 1), :]
            contrib[pl.ds(r, 1), :] = jnp.where((li >= 0) & (li < rows), row, 0.0)
            return 0

        lax.fori_loop(0, count, one, 0, unroll=8)

    def piece(d, j):
        return j if d == 0 else 31 - j

    def scatter(d, j):
        c = piece(d, j)
        return remote(t.at[c], t.at[c], s_send.at[d, j], s_recv.at[d, j], nxt[d])

    nblocks = len(BLOCKS)
    first_of = [15 - sum(BLOCKS[:b]) for b in range(nblocks)]

    def fill(b):
        if b >= nblocks:
            return

        @pl.when(z == 0)
        def _():
            for d in (0, 1):
                base = HALF * (first_of[b] - BLOCKS[b] + 1 if d == 0 else 31 - first_of[b])

                def one(i, _):
                    r = base + i
                    row = mat[pl.ds(jnp.clip(two_smem[r] & (NB - 1), 0, rows - 1), 1), :]
                    t[r // HALF, pl.ds(r % HALF, 1), :] = row
                    return 0

                lax.fori_loop(0, HALF * BLOCKS[b], one, 0, unroll=8)

    def pass_on(step):
        for d in (0, 1):
            b = step - dist[d]
            first, count = jnp.int32(0), jnp.int32(0)
            for i in range(nblocks):
                first = jnp.where(b == i, first_of[i], first)
                count = jnp.where(b == i, BLOCKS[i], count)
            for u in range(max(BLOCKS)):
                j = jnp.clip(first - u, 0, 15)
                valid = u < count

                @pl.when(valid & (dist[d] >= 1) & (dist[d] <= reach(j)))
                def _():
                    scatter(d, j).wait_recv()

                @pl.when(valid & (dist[d] < reach(j)))
                def _():
                    scatter(d, j).start()

    def order():
        loads[1].wait()
        kk = lax.broadcasted_iota(jnp.int32, (NB, NB), 0)
        perm = (kk == (one_ref[...] & (NB - 1))).astype(F32).astype(BF16)
        hi, lo = split(linv[...])
        lhi[...] = dot(hi, perm).astype(BF16)
        llo[...] = dot(lo, perm).astype(BF16)

    def base():
        for r in range(0, rows, 256):
            qq = lax.broadcasted_iota(jnp.int32, (256, WIN), 0) + r
            hit = (qq + off == tgt_ref[...]).astype(F32)
            hot[pl.ds(r, 256), :] = hit.astype(BF16)
            gone = jnp.max(hit, axis=1, keepdims=True) > 0.0
            top = (lax.broadcasted_iota(jnp.int32, (256, 1), 0) + r < NB) & (z == 0)
            out[pl.ds(r, 256), :] = jnp.where(gone | top, 0.0, mat[pl.ds(r, 256), :])

    def weights(r):
        a = pall[:, :, :, r:r + 256].reshape(NB, 256)
        ahi, alo = split(a)
        acc = dot(ahi, lhi[...], 0) + dot(ahi, llo[...], 0) + dot(alo, lhi[...], 0)
        qq = lax.broadcasted_iota(jnp.int32, (256, NB), 0) + r
        own = (qq == (one_ref[...] & (NB - 1))) & (z == 0)
        acc = acc - own.astype(F32)
        hi, lo = split(acc)
        whi[pl.ds(r, 256), :] = hi
        wlo[pl.ds(r, 256), :] = lo

    def product(k, c):
        qhi, qlo = split(q[k // CH:k // CH + 8, :, c:c + 256].reshape(256, 256))
        a, b = whi[:, k:k + 256], wlo[:, k:k + 256]
        return dot(a, qhi) + dot(a, qlo) + dot(b, qhi)

    def update(c):
        out[:, c:c + 256] -= product(0, c)

    def finish(c):
        thi, tlo = split(t[pl.ds(window(z), 16), :, c:c + 256].reshape(WIN, 256))
        out[:, c:c + 256] += dot(hot[...], thi) + dot(hot[...], tlo) - product(256, c)

    def check():
        i = lax.broadcasted_iota(jnp.int32, (1, NB), 1)

        def block(v):
            return sum((v >= rows * b).astype(jnp.int32) for b in range(1, NZ))

        away = (block(one_ref[...] >> BITS) - z - i // CH + 2 * NZ + 12) % NZ - 8
        late = i % CH >= HALF
        good = (jnp.abs(away) <= 1) | ((away == -2) & ~late) | ((away == 2) & late)
        tgt = two_ref[...] >> BITS
        dest = block(tgt)
        hops = jnp.where(i < NB // 2, dest, NZ - dest)
        near = jnp.where(i < NB // 2, i, NB - 1 - i) // HALF
        inside = i - HALF * window(dest)
        good &= (tgt < NB) | ((inside >= 0) & (inside < WIN) & ((dest == 0) | (hops <= reach(near))))
        misfit[0] = jnp.max(jnp.where(good, 0, 1))

    stripes = list(range(0, cols, 256))
    later = {1: [order], 2: [base, check]}
    for i in range(3):
        later[3 + i] = [functools.partial(weights, 256 * i)]
    for i, c in enumerate(stripes):
        later[6 + i] = [functools.partial(update, c)]

    for i in range(nx - 1):
        pan_x(i).start()
    loads[0].wait()
    take_rows(0, HALF)
    take_rows(112, HALF)
    home(0, 0).start()
    home(1, 0).start()
    fill(0)
    pass_on(0)
    take_rows(16, CH)
    take_rows(80, CH)

    home(0, 0).wait_recv()
    contrib[pl.ds(80, HALF), :] += left1[...]
    home(0, 1).start()
    home(1, 0).wait_recv()
    contrib[pl.ds(32, HALF), :] += right1[...]
    home(1, 1).start()
    fill(1)
    pass_on(1)
    take_rows(48, CH)
    fill(2)
    loads[2].wait()
    for i in range(nx - 1):
        pan_x(i).wait_recv()
    for i in range(ny - 1):
        pan_y(i).start()

    home(0, 1).wait_recv()
    home(1, 1).wait_recv()
    q[4] = contrib[pl.ds(48, CH), :] + left2[...] + right2[...]
    for k in range(1, KSTEP + 1):
        ring(k)
        pass_on(1 + k)
        fill(2 + k)
        if k == 2:
            for i in range(ny - 1):
                pan_y(i).wait_recv()
            if cpart:
                pan_c().start()
        if k == 3 and cpart:
            pan_c().wait_recv()
        for f in later.pop(k, []):
            f()
    for fs in later.values():
        for f in fs:
            f()
    for step in range(KSTEP + 2, nblocks + 10):
        pass_on(step)
    ring(KSTEP + 1)
    for c in stripes:
        finish(c)

    for d in (0, 1):
        home(d, 0).wait_send()
        home(d, 1).wait_send()
        for k in range(1, KSTEP + 1):
            for u in (0, 1):
                on(senders(d, k, u), lambda: gather(d, k, u).wait_send())

        def sent(j, _):
            @pl.when(dist[d] < reach(j))
            def _():
                scatter(d, j).wait_send()

            return 0

        lax.fori_loop(0, 16, sent, 0)
    for i in range(nx - 1):
        pan_x(i).wait_send()
    for i in range(ny - 1):
        pan_y(i).wait_send()
    if cpart:
        pan_c().wait_send()


def plan(touched, anchor, rows, z):
    idx = jnp.arange(NB, dtype=jnp.int32)
    src, owner = anchor[:NB], anchor[:NB] // rows
    tgt, top = touched[NB:], anchor[NB:]

    def rank(group):
        key = group * NB + idx
        return jnp.sum((key[None, :] < key[:, None]).astype(jnp.int32), axis=1)

    def place(pos, values):
        return jnp.sum(jnp.where(pos[:, None] == idx[None, :], values[:, None], 0), axis=0)

    r, s = rank(owner), rank(tgt)
    here = (r - CH * z + 4 * CH) % NB
    one = place(here, src * NB + idx)
    two = place(s, tgt * NB + jnp.clip(top, 0, NB - 1))
    goes = two >> BITS
    before = jnp.concatenate([jnp.full((1,), -1, jnp.int32), goes[:-1]])
    goes = jnp.where((goes < NB) | (goes == before), -1, goes)
    return one, two, lax.dynamic_slice_in_dim(goes, HALF * window(z), WIN)


def plain(matrix, panel_t, l_inverse, touched, anchor):
    rows = matrix.shape[0]
    offset = lax.axis_index("prow") * rows
    local = anchor - offset
    owned = (local >= 0) & (local < rows)
    picked = jnp.where(owned[:, None], matrix[jnp.clip(local, 0, rows - 1)], 0.0)

    def ring(axis, init):
        n = lax.axis_size(axis)
        pairs = [(i, (i + 1) % n) for i in range(n)]
        return n, lambda v: lax.ppermute(v, axis, pairs), init

    n, shift, _ = ring("prow", None)

    def add(_, carry):
        part, total = carry
        part = shift(part)
        return part, total + part

    _, moved = lax.fori_loop(0, n - 1, add, (picked, picked))
    m, shift_p, _ = ring("pcol", None)
    me = lax.axis_index("pcol")
    wide = jnp.zeros((m,) + panel_t.shape, panel_t.dtype).at[me].set(panel_t)

    def put(i, carry):
        part, whole = carry
        return shift_p(part), lax.dynamic_update_index_in_dim(whole, part, (me - 1 - i) % m, 0)

    _, wide = lax.fori_loop(0, m - 1, put, (shift_p(panel_t), wide))
    high = functools.partial(jnp.dot, precision=lax.Precision.HIGHEST, preferred_element_type=F32)
    upper = high(l_inverse, moved[:NB])
    target = touched - offset
    target = jnp.where((target >= 0) & (target < rows), target, rows)
    lands = jnp.full((rows,), -1, jnp.int32).at[target].set(jnp.arange(2 * NB, dtype=jnp.int32), mode="drop")
    permuted = jnp.where((lands >= 0)[:, None], moved[jnp.clip(lands, 0, 2 * NB - 1)], matrix)
    return permuted - high(wide.reshape(NB, rows).T, upper)


def fast(shape, matrix, panel_t, l_inverse, one, two, tgt):
    rows, cols = matrix.shape
    ny, nx, nc = shape
    vmem, smem = pl.BlockSpec(memory_space=pltpu.VMEM), pl.BlockSpec(memory_space=pltpu.SMEM)
    hbm = pl.BlockSpec(memory_space=pl.ANY)
    npan = max(nx + ny - 1, 1)
    dma = pltpu.SemaphoreType.DMA
    return pl.pallas_call(
        functools.partial(kernel, shape),
        out_shape=(pltpu.VMEM((rows, cols), F32), jax.ShapeDtypeStruct((1,), jnp.int32)),
        in_specs=[smem, smem, vmem, vmem, vmem, hbm, hbm, hbm],
        out_specs=(vmem, smem),
        scratch_shapes=[
            pltpu.VMEM((rows, cols), F32),
            pltpu.VMEM((NB, NB), F32),
            pltpu.VMEM((128, cols), F32),
            pltpu.VMEM((HALF, cols), F32),
            pltpu.VMEM((HALF, cols), F32),
            pltpu.VMEM((CH, cols), F32),
            pltpu.VMEM((CH, cols), F32),
            pltpu.VMEM((NZ, CH, cols), F32),
            pltpu.VMEM((32, HALF, cols), F32),
            pltpu.VMEM((ny * nx, nc, panel_t.shape[0], rows), F32),
            pltpu.VMEM((NB, NB), BF16),
            pltpu.VMEM((NB, NB), BF16),
            pltpu.VMEM((rows, NB), BF16),
            pltpu.VMEM((rows, NB), BF16),
            pltpu.VMEM((rows, WIN), BF16),
            dma((4,)), dma((4,)), dma((4 * KSTEP,)), dma((4 * KSTEP,)),
            dma((2, 16)), dma((2, 16)), dma((npan,)), dma((npan,)), dma((3,)),
        ],
        compiler_params=pltpu.CompilerParams(
            collective_id=0, has_side_effects=True, vmem_limit_bytes=60 * 2**20
        ),
    )(one, two, one.reshape(1, NB), two.reshape(1, NB), tgt.reshape(1, WIN), matrix, panel_t, l_inverse)


def body(shape, matrix, panel, l_inverse, touched, anchor):
    z = lax.axis_index("prow")
    one, two, tgt = plan(touched, anchor, matrix.shape[0], z)
    panel_t = panel.T
    done, misfit = fast(shape, matrix, panel_t, l_inverse, one, two, tgt)
    return lax.cond(misfit[0] == 0, lambda: done, lambda: plain(matrix, panel_t, l_inverse, touched, anchor))


def solution(mesh):
    n = mesh.shape["pcol"]
    shape = (4, 4, 2) if n == 32 else (1, n, 1)
    in_specs = (P("prow", "pcol"), P("prow", "pcol"), P(), P(), P())
    return jax.shard_map(
        functools.partial(body, shape), mesh=mesh, in_specs=in_specs, out_specs=P("prow", "pcol"), check_vma=False
    )
```

```python
import functools

import jax
import jax.numpy as jnp
from jax import lax
from jax.experimental import pallas as pl
from jax.experimental.pallas import tpu as pltpu
from jax.sharding import PartitionSpec as P

MESH = pl.DeviceIdType.MESH
NZ = 16
CH = 32
HALF = 16
WIN = 256
NB = NZ * CH
BITS = 9
F32, BF16 = jnp.float32, jnp.bfloat16


def reach(j):
    return (j + 1) // 2 + 2


UPWARDS = [(7, 7)] * 5 + [(8, 8)] * 3 + [(7, 7)] * 8
KSTEP = max(max(a, NZ - 1 - a) for p in UPWARDS for a in p)
BLOCKS = [2] * 8


def window(z):
    return jnp.clip(2 * z - 7, 0, 16)


def split(x):
    hi = x.astype(BF16)
    return hi, (x - hi.astype(F32)).astype(BF16)


def dot(a, b, ca=1):
    return lax.dot_general(a, b, (((ca,), (0,)), ((), ())), preferred_element_type=F32)


def kernel(
    shape, one_smem, two_smem, one_ref, two_ref, mat_hbm, pan, linv_hbm, out, misfit,
    mat, linv, contrib, left1, right1, left2, right2, q, t, pall, lhi, llo, whi, wlo, hot,
    p_send, p_recv, g_send, g_recv, s_send, s_recv, pan_send, pan_recv, load,
):
    ny, nx, nc = shape
    rows, cols = mat.shape
    z = lax.axis_index("prow")
    w = lax.axis_index("pcol")
    core, x, y = w % nc, (w // nc) % nx, w // (nc * nx)
    off = z * rows
    up, down = (z + 1) % NZ, (z + NZ - 1) % NZ
    dist = (z, (NZ - z) % NZ)
    nxt = ({"prow": up}, {"prow": down})

    def pcol(yy, xx, cc):
        return {"pcol": (yy * nx + xx) * nc + cc}

    xpart = [pcol(y, (x + d) % nx, core) for d in range(1, nx)]
    ypart = [pcol((y + d) % ny, x, core) for d in range(1, ny)]
    cpart = [pcol(y, x, 1 - core)] if nc == 2 else []
    partners = list(nxt) + xpart + ypart + cpart
    mine = y * nx + x

    loads = [
        pltpu.make_async_copy(mat_hbm, mat, load.at[0]),
        pltpu.make_async_copy(pan, pall.at[mine, core], load.at[1]),
        pltpu.make_async_copy(linv_hbm, linv, load.at[2]),
    ]
    for c in loads:
        c.start()

    barrier = pltpu.get_barrier_semaphore()
    for dev in partners:
        pl.semaphore_signal(barrier, inc=1, device_id=dev, device_id_type=MESH)
    pl.semaphore_wait(barrier, len(partners))

    def remote(src, dst, ss, rs, dev):
        return pltpu.make_async_remote_copy(
            src_ref=src, dst_ref=dst, send_sem=ss, recv_sem=rs, device_id=dev, device_id_type=MESH
        )

    def on(devices, act):
        if len(devices) == NZ:
            act()
            return
        starts = [i for i in sorted(devices) if (i - 1) % NZ not in devices]
        hit = None
        for i in starts:
            n = 1
            while (i + n) % NZ in devices:
                n += 1
            one = (z + NZ - i) % NZ < n
            hit = one if hit is None else hit | one
        if hit is not None:
            pl.when(hit)(act)

    def pan_x(i):
        return remote(pan, pall.at[mine, core], pan_send.at[i], pan_recv.at[i], xpart[i])

    def pan_y(i):
        rowset = pall.at[pl.ds(y * nx, nx), core]
        return remote(rowset, rowset, pan_send.at[nx - 1 + i], pan_recv.at[nx - 1 + i], ypart[i])

    def pan_c():
        k = nx + ny - 2
        return remote(pall.at[:, core], pall.at[:, core], pan_send.at[k], pan_recv.at[k], cpart[0])

    def home(d, k):
        if k == 0:
            src = contrib.at[pl.ds(112, HALF)] if d == 0 else contrib.at[pl.ds(0, HALF)]
            dst = (left1, right1)[d]
        else:
            src = contrib.at[pl.ds(80, CH)] if d == 0 else contrib.at[pl.ds(16, CH)]
            dst = (left2, right2)[d]
        i = 2 * k + d
        return remote(src, dst, p_send.at[i], p_recv.at[i], nxt[d])

    def gather(d, k, u):
        src, dst = ((5 - k) % NZ, (4 - k) % NZ) if d == 0 else (3 + k, 4 + k)
        part = pl.ds(HALF * u, HALF)
        i = (2 * (k - 1) + d) * 2 + u
        return remote(q.at[src, part], q.at[dst, part], g_send.at[i], g_recv.at[i], nxt[d])

    def senders(d, k, u):
        keep = set()
        for i in range(NZ):
            h = (i - (k - 1)) % NZ if d == 0 else (i + (k - 1)) % NZ
            far = UPWARDS[h][u] if d == 0 else NZ - 1 - UPWARDS[h][u]
            if k <= far:
                keep.add(i)
        return keep

    def ring(k):
        for u in (0, 1):
            for d in (0, 1):
                if k > 1:
                    came = {(i + (1 if d == 0 else -1)) % NZ for i in senders(d, k - 1, u)}
                    on(came, lambda: gather(d, k - 1, u).wait_recv())
                if k <= KSTEP:
                    on(senders(d, k, u), lambda: gather(d, k, u).start())

    def take_rows(first, count):
        def one(i, _):
            r = first + i
            li = (one_smem[80 + r] >> BITS) - off
            row = mat[pl.ds(jnp.clip(li, 0, rows - 1), 1), :]
            contrib[pl.ds(r, 1), :] = jnp.where((li >= 0) & (li < rows), row, 0.0)
            return 0

        lax.fori_loop(0, count, one, 0, unroll=8)

    def piece(d, j):
        return j if d == 0 else 31 - j

    def scatter(d, j):
        c = piece(d, j)
        return remote(t.at[c], t.at[c], s_send.at[d, j], s_recv.at[d, j], nxt[d])

    nblocks = len(BLOCKS)
    first_of = [15 - sum(BLOCKS[:b]) for b in range(nblocks)]

    def fill(b):
        if b >= nblocks:
            return

        @pl.when(z == 0)
        def _():
            for d in (0, 1):
                base = HALF * (first_of[b] - BLOCKS[b] + 1 if d == 0 else 31 - first_of[b])

                def one(i, _):
                    r = base + i
                    row = mat[pl.ds(jnp.clip(two_smem[r] & (NB - 1), 0, rows - 1), 1), :]
                    t[r // HALF, pl.ds(r % HALF, 1), :] = row
                    return 0

                lax.fori_loop(0, HALF * BLOCKS[b], one, 0, unroll=8)

    def pass_on(step):
        for d in (0, 1):
            b = step - dist[d]
            first, count = jnp.int32(0), jnp.int32(0)
            for i in range(nblocks):
                first = jnp.where(b == i, first_of[i], first)
                count = jnp.where(b == i, BLOCKS[i], count)
            for u in range(max(BLOCKS)):
                j = jnp.clip(first - u, 0, 15)
                valid = u < count

                @pl.when(valid & (dist[d] >= 1) & (dist[d] <= reach(j)))
                def _():
                    scatter(d, j).wait_recv()

                @pl.when(valid & (dist[d] < reach(j)))
                def _():
                    scatter(d, j).start()

    def order():
        loads[2].wait()
        kk = lax.broadcasted_iota(jnp.int32, (NB, NB), 0)
        perm = (kk == (one_ref[...] & (NB - 1))).astype(F32).astype(BF16)
        hi, lo = split(linv[...])
        lhi[...] = dot(hi, perm).astype(BF16)
        llo[...] = dot(lo, perm).astype(BF16)

    def base():
        tgt = two_ref[...] >> BITS
        i = lax.broadcasted_iota(jnp.int32, (1, NB), 1)
        again = (tgt == pltpu.roll(tgt, 1, 1)) & (i > 0)
        tgt = jnp.where(again | (tgt < NB), -1, tgt)
        tgt = pltpu.roll(tgt, (NB - HALF * window(z)) % NB, 1)[:, :WIN]
        for r in range(0, rows, 256):
            qq = lax.broadcasted_iota(jnp.int32, (256, WIN), 0) + r
            hit = (qq + off == tgt).astype(F32)
            hot[pl.ds(r, 256), :] = hit.astype(BF16)
            gone = jnp.max(hit, axis=1, keepdims=True) > 0.0
            top = (lax.broadcasted_iota(jnp.int32, (256, 1), 0) + r < NB) & (z == 0)
            out[pl.ds(r, 256), :] = jnp.where(gone | top, 0.0, mat[pl.ds(r, 256), :])

    def weights(r):
        a = pall[:, :, :, r:r + 256].reshape(NB, 256)
        ahi, alo = split(a)
        acc = dot(ahi, lhi[...], 0) + dot(ahi, llo[...], 0) + dot(alo, lhi[...], 0)
        qq = lax.broadcasted_iota(jnp.int32, (256, NB), 0) + r
        own = (qq == (one_ref[...] & (NB - 1))) & (z == 0)
        acc = acc - own.astype(F32)
        hi, lo = split(acc)
        whi[pl.ds(r, 256), :] = hi
        wlo[pl.ds(r, 256), :] = lo

    def product(k, c):
        qhi, qlo = split(q[k // CH:k // CH + 8, :, c:c + 256].reshape(256, 256))
        a, b = whi[:, k:k + 256], wlo[:, k:k + 256]
        return dot(a, qhi) + dot(a, qlo) + dot(b, qhi)

    def update(c):
        out[:, c:c + 256] -= product(0, c)

    def finish(c):
        i = window(z) + lax.broadcasted_iota(jnp.int32, (WIN, 1), 0) // HALF
        near = jnp.where(i < 16, i, 31 - i)
        came = jnp.where(i < 16, dist[0], dist[1]) <= reach(near)
        thi, tlo = split(jnp.where(came, t[pl.ds(window(z), 16), :, c:c + 256].reshape(WIN, 256), 0.0))
        out[:, c:c + 256] += dot(hot[...], thi) + dot(hot[...], tlo) - product(256, c)

    def check():
        i = lax.broadcasted_iota(jnp.int32, (1, NB), 1)

        def block(v):
            return sum((v >= rows * b).astype(jnp.int32) for b in range(1, NZ))

        away = (block(one_ref[...] >> BITS) - z - i // CH + 2 * NZ + 12) % NZ - 8
        late = i % CH >= HALF
        good = (jnp.abs(away) <= 1) | ((away == -2) & ~late) | ((away == 2) & late)
        tgt = two_ref[...] >> BITS
        dest = block(tgt)
        hops = jnp.where(i < NB // 2, dest, NZ - dest)
        near = jnp.where(i < NB // 2, i, NB - 1 - i) // HALF
        inside = i - HALF * window(dest)
        good &= (tgt < NB) | ((inside >= 0) & (inside < WIN) & ((dest == 0) | (hops <= reach(near))))
        misfit[0] = jnp.max(jnp.where(good, 0, 1))

    stripes = list(range(0, cols, 256))
    later = {1: [order], 2: [base, check]}
    for i in range(3):
        later[3 + i] = [functools.partial(weights, 256 * i)]
    for i, c in enumerate(stripes):
        later[6 + i] = [functools.partial(update, c)]

    for i in range(nx - 1):
        pan_x(i).start()
    loads[0].wait()
    take_rows(0, HALF)
    take_rows(112, HALF)
    home(0, 0).start()
    home(1, 0).start()
    fill(0)
    pass_on(0)
    take_rows(16, CH)
    take_rows(80, CH)
    loads[1].wait()

    home(0, 0).wait_recv()
    contrib[pl.ds(80, HALF), :] += left1[...]
    home(0, 1).start()
    home(1, 0).wait_recv()
    contrib[pl.ds(32, HALF), :] += right1[...]
    home(1, 1).start()
    fill(1)
    pass_on(1)
    take_rows(48, CH)
    fill(2)
    for i in range(nx - 1):
        pan_x(i).wait_recv()
    for i in range(ny - 1):
        pan_y(i).start()

    home(0, 1).wait_recv()
    home(1, 1).wait_recv()
    q[4] = contrib[pl.ds(48, CH), :] + left2[...] + right2[...]
    for k in range(1, KSTEP + 1):
        ring(k)
        pass_on(1 + k)
        fill(2 + k)
        if k == 2:
            for i in range(ny - 1):
                pan_y(i).wait_recv()
            if cpart:
                pan_c().start()
        if k == 3 and cpart:
            pan_c().wait_recv()
        for f in later.pop(k, []):
            f()
    for fs in later.values():
        for f in fs:
            f()
    for step in range(KSTEP + 2, nblocks + 10):
        pass_on(step)
    ring(KSTEP + 1)
    for c in stripes:
        finish(c)

    for d in (0, 1):
        home(d, 0).wait_send()
        home(d, 1).wait_send()
        for k in range(1, KSTEP + 1):
            for u in (0, 1):
                on(senders(d, k, u), lambda: gather(d, k, u).wait_send())

        def sent(j, _):
            @pl.when(dist[d] < reach(j))
            def _():
                scatter(d, j).wait_send()

            return 0

        lax.fori_loop(0, 16, sent, 0)
    for i in range(nx - 1):
        pan_x(i).wait_send()
    for i in range(ny - 1):
        pan_y(i).wait_send()
    if cpart:
        pan_c().wait_send()


def plan(touched, anchor, rows, z):
    idx = jnp.arange(NB, dtype=jnp.int32)
    src, owner = anchor[:NB], anchor[:NB] // rows
    tgt, top = touched[NB:], anchor[NB:]

    def rank(group):
        key = group * NB + idx
        return jnp.sum((key[None, :] < key[:, None]).astype(jnp.int32), axis=1)

    def place(pos, values):
        return jnp.sum(jnp.where(pos[:, None] == idx[None, :], values[:, None], 0), axis=0)

    r, s = rank(owner), rank(tgt)
    here = (r - CH * z + 4 * CH) % NB
    one = place(here, src * NB + idx)
    two = place(s, tgt * NB + jnp.clip(top, 0, NB - 1))
    return one, two


def plain(matrix, panel_t, l_inverse, touched, anchor):
    rows = matrix.shape[0]
    offset = lax.axis_index("prow") * rows
    local = anchor - offset
    owned = (local >= 0) & (local < rows)
    picked = jnp.where(owned[:, None], matrix[jnp.clip(local, 0, rows - 1)], 0.0)

    def ring(axis, init):
        n = lax.axis_size(axis)
        pairs = [(i, (i + 1) % n) for i in range(n)]
        return n, lambda v: lax.ppermute(v, axis, pairs), init

    n, shift, _ = ring("prow", None)

    def add(_, carry):
        part, total = carry
        part = shift(part)
        return part, total + part

    _, moved = lax.fori_loop(0, n - 1, add, (picked, picked))
    m, shift_p, _ = ring("pcol", None)
    me = lax.axis_index("pcol")
    wide = jnp.zeros((m,) + panel_t.shape, panel_t.dtype).at[me].set(panel_t)

    def put(i, carry):
        part, whole = carry
        return shift_p(part), lax.dynamic_update_index_in_dim(whole, part, (me - 1 - i) % m, 0)

    _, wide = lax.fori_loop(0, m - 1, put, (shift_p(panel_t), wide))
    high = functools.partial(jnp.dot, precision=lax.Precision.HIGHEST, preferred_element_type=F32)
    upper = high(l_inverse, moved[:NB])
    target = touched - offset
    target = jnp.where((target >= 0) & (target < rows), target, rows)
    lands = jnp.full((rows,), -1, jnp.int32).at[target].set(jnp.arange(2 * NB, dtype=jnp.int32), mode="drop")
    permuted = jnp.where((lands >= 0)[:, None], moved[jnp.clip(lands, 0, 2 * NB - 1)], matrix)
    return permuted - high(wide.reshape(NB, rows).T, upper)


def fast(shape, matrix, panel_t, l_inverse, one, two):
    rows, cols = matrix.shape
    ny, nx, nc = shape
    vmem, smem = pl.BlockSpec(memory_space=pltpu.VMEM), pl.BlockSpec(memory_space=pltpu.SMEM)
    hbm = pl.BlockSpec(memory_space=pl.ANY)
    npan = max(nx + ny - 1, 1)
    dma = pltpu.SemaphoreType.DMA
    return pl.pallas_call(
        functools.partial(kernel, shape),
        out_shape=(pltpu.VMEM((rows, cols), F32), pltpu.SMEM((1,), jnp.int32)),
        in_specs=[smem, smem, vmem, vmem, hbm, hbm, hbm],
        out_specs=(vmem, smem),
        scratch_shapes=[
            pltpu.VMEM((rows, cols), F32),
            pltpu.VMEM((NB, NB), F32),
            pltpu.VMEM((128, cols), F32),
            pltpu.VMEM((HALF, cols), F32),
            pltpu.VMEM((HALF, cols), F32),
            pltpu.VMEM((CH, cols), F32),
            pltpu.VMEM((CH, cols), F32),
            pltpu.VMEM((NZ, CH, cols), F32),
            pltpu.VMEM((32, HALF, cols), F32),
            pltpu.VMEM((ny * nx, nc, panel_t.shape[0], rows), F32),
            pltpu.VMEM((NB, NB), BF16),
            pltpu.VMEM((NB, NB), BF16),
            pltpu.VMEM((rows, NB), BF16),
            pltpu.VMEM((rows, NB), BF16),
            pltpu.VMEM((rows, WIN), BF16),
            dma((4,)), dma((4,)), dma((4 * KSTEP,)), dma((4 * KSTEP,)),
            dma((2, 16)), dma((2, 16)), dma((npan,)), dma((npan,)), dma((3,)),
        ],
        compiler_params=pltpu.CompilerParams(
            collective_id=0, has_side_effects=True, vmem_limit_bytes=40 * 2**20
        ),
    )(one, two, one.reshape(1, NB), two.reshape(1, NB), matrix, panel_t, l_inverse)


def body(shape, matrix, panel, l_inverse, touched, anchor):
    z = lax.axis_index("prow")
    one, two = plan(touched, anchor, matrix.shape[0], z)
    panel_t = panel.T
    done, misfit = fast(shape, matrix, panel_t, l_inverse, one, two)
    return lax.cond(misfit[0] == 0, lambda: done, lambda: plain(matrix, panel_t, l_inverse, touched, anchor))


def solution(mesh):
    n = mesh.shape["pcol"]
    shape = (4, 4, 2) if n == 32 else (1, n, 1)
    in_specs = (P("prow", "pcol"), P("prow", "pcol"), P(), P(), P())
    return jax.shard_map(
        functools.partial(body, shape), mesh=mesh, in_specs=in_specs, out_specs=P("prow", "pcol"), check_vma=False
    )
```

```python
import functools

import jax
import jax.numpy as jnp
from jax import lax
from jax.experimental import pallas as pl
from jax.experimental.pallas import tpu as pltpu
from jax.sharding import PartitionSpec as P

MESH = pl.DeviceIdType.MESH
NZ = 16
CH = 32
HALF = 16
WIN = 256
NB = NZ * CH
BITS = 9
F32, BF16 = jnp.float32, jnp.bfloat16


def reach(j):
    return (j + 1) // 2 + 2


UPWARDS = (
    [(7, 7)] * 5 + [(8, 8)] * 3 + [(7, 7)] * 8,
    [(8, 8), (10, 10), (10, 10), (7, 10), (10, 10), (10, 10), (9, 9), (8, 8),
     (8, 8), (7, 7), (5, 5), (5, 5), (5, 5), (5, 6), (6, 6), (7, 7)],
)
KSTEP = max(max(a, NZ - 1 - a) for table in UPWARDS for p in table for a in p)
BLOCKS = ([2] * 8 + [0, 0], [1] * 4 + [2] * 6)
NBLOCKS = len(BLOCKS[0])
FIRST = tuple([15 - sum(table[:b]) for b in range(NBLOCKS)] for table in BLOCKS)


def window(z):
    return jnp.clip(2 * z - 7, 0, 16)


def split(x):
    hi = x.astype(BF16)
    return hi, (x - hi.astype(F32)).astype(BF16)


def dot(a, b, ca=1):
    return lax.dot_general(a, b, (((ca,), (0,)), ((), ())), preferred_element_type=F32)


def kernel(
    shape, one_smem, two_smem, one_ref, two_ref, mat_hbm, pan, linv_hbm, out, misfit,
    mat, linv, contrib, left1, right1, left2, right2, q, t, pall, lhi, llo, whi, wlo, hot,
    p_send, p_recv, g_send, g_recv, s_send, s_recv, pan_send, pan_recv, load,
):
    ny, nx, nc = shape
    rows, cols = mat.shape
    z = lax.axis_index("prow")
    w = lax.axis_index("pcol")
    core, x, y = w % nc, (w // nc) % nx, w // (nc * nx)
    off = z * rows
    up, down = (z + 1) % NZ, (z + NZ - 1) % NZ
    dist = (z, (NZ - z) % NZ)
    nxt = ({"prow": up}, {"prow": down})

    def pcol(yy, xx, cc):
        return {"pcol": (yy * nx + xx) * nc + cc}

    xpart = [pcol(y, (x + d) % nx, core) for d in range(1, nx)]
    ypart = [pcol((y + d) % ny, x, core) for d in range(1, ny)]
    cpart = [pcol(y, x, 1 - core)] if nc == 2 else []
    partners = list(nxt) + xpart + ypart + cpart
    mine = y * nx + x

    loads = [
        pltpu.make_async_copy(mat_hbm, mat, load.at[0]),
        pltpu.make_async_copy(pan, pall.at[mine, core], load.at[1]),
        pltpu.make_async_copy(linv_hbm, linv, load.at[2]),
    ]
    for c in loads:
        c.start()

    barrier = pltpu.get_barrier_semaphore()
    for dev in partners:
        pl.semaphore_signal(barrier, inc=1, device_id=dev, device_id_type=MESH)
    pl.semaphore_wait(barrier, len(partners))

    def remote(src, dst, ss, rs, dev):
        return pltpu.make_async_remote_copy(
            src_ref=src, dst_ref=dst, send_sem=ss, recv_sem=rs, device_id=dev, device_id_type=MESH
        )

    def among(devices):
        hit = None
        for i in sorted(devices):
            if (i - 1) % NZ in devices:
                continue
            n = 1
            while (i + n) % NZ in devices:
                n += 1
            one = (z + NZ - i) % NZ < n
            hit = one if hit is None else hit | one
        return hit

    def on(devices, act):
        sets = [devices(c) for c in range(nc)]
        if all(len(s) == NZ for s in sets):
            act()
        elif all(s == sets[0] for s in sets):
            if sets[0]:
                pl.when(among(sets[0]))(act)
        else:
            hit = None
            for c, s in enumerate(sets):
                if s:
                    one = core == c if len(s) == NZ else (core == c) & among(s)
                    hit = one if hit is None else hit | one
            pl.when(hit)(act)

    def by_core(table, b):
        return jnp.where(core == 0, table[0][b], table[1][b])

    def pan_x(i):
        return remote(pan, pall.at[mine, core], pan_send.at[i], pan_recv.at[i], xpart[i])

    def pan_y(i):
        rowset = pall.at[pl.ds(y * nx, nx), core]
        return remote(rowset, rowset, pan_send.at[nx - 1 + i], pan_recv.at[nx - 1 + i], ypart[i])

    def pan_c():
        k = nx + ny - 2
        return remote(pall.at[:, core], pall.at[:, core], pan_send.at[k], pan_recv.at[k], cpart[0])

    def home(d, k):
        if k == 0:
            src = contrib.at[pl.ds(112, HALF)] if d == 0 else contrib.at[pl.ds(0, HALF)]
            dst = (left1, right1)[d]
        else:
            src = contrib.at[pl.ds(80, CH)] if d == 0 else contrib.at[pl.ds(16, CH)]
            dst = (left2, right2)[d]
        i = 2 * k + d
        return remote(src, dst, p_send.at[i], p_recv.at[i], nxt[d])

    def gather(d, k, u):
        src, dst = ((5 - k) % NZ, (4 - k) % NZ) if d == 0 else (3 + k, 4 + k)
        part = pl.ds(HALF * u, HALF)
        i = (2 * (k - 1) + d) * 2 + u
        return remote(q.at[src, part], q.at[dst, part], g_send.at[i], g_recv.at[i], nxt[d])

    def senders(d, k, u, c):
        keep = set()
        for i in range(NZ):
            h = (i - (k - 1)) % NZ if d == 0 else (i + (k - 1)) % NZ
            far = UPWARDS[c][h][u] if d == 0 else NZ - 1 - UPWARDS[c][h][u]
            if k <= far:
                keep.add(i)
        return keep

    def ring(k):
        for u in (0, 1):
            for d in (0, 1):
                if k > 1:
                    came = lambda c: {(i + (1 if d == 0 else -1)) % NZ for i in senders(d, k - 1, u, c)}
                    on(came, lambda: gather(d, k - 1, u).wait_recv())
                if k <= KSTEP:
                    on(functools.partial(senders, d, k, u), lambda: gather(d, k, u).start())

    def take_rows(first, count):
        def one(i, _):
            r = first + i
            li = (one_smem[80 + r] >> BITS) - off
            row = mat[pl.ds(jnp.clip(li, 0, rows - 1), 1), :]
            contrib[pl.ds(r, 1), :] = jnp.where((li >= 0) & (li < rows), row, 0.0)
            return 0

        lax.fori_loop(0, count, one, 0, unroll=8)

    def piece(d, j):
        return j if d == 0 else 31 - j

    def scatter(d, j):
        c = piece(d, j)
        return remote(t.at[c], t.at[c], s_send.at[d, j], s_recv.at[d, j], nxt[d])

    def fill(b):
        if b >= NBLOCKS or not any(table[b] for table in BLOCKS):
            return

        @pl.when(z == 0)
        def _():
            def both(v, _):
                c = jnp.where(v % 2 == 0, by_core(FIRST, b) - v // 2, 31 - by_core(FIRST, b) + v // 2)

                def one(i, _):
                    row = mat[pl.ds(jnp.clip(two_smem[c * HALF + i] & (NB - 1), 0, rows - 1), 1), :]
                    t[c, pl.ds(i, 1), :] = row
                    return 0

                return lax.fori_loop(0, HALF, one, 0, unroll=8)

            lax.fori_loop(0, 2 * by_core(BLOCKS, b), both, 0)

    def pass_on(step):
        for d in (0, 1):
            b = step - dist[d]
            first, count = jnp.int32(0), jnp.int32(0)
            for i in range(NBLOCKS):
                first = jnp.where(b == i, by_core(FIRST, i), first)
                count = jnp.where(b == i, by_core(BLOCKS, i), count)
            for u in range(2):
                j = jnp.clip(first - u, 0, 15)
                valid = u < count

                @pl.when(valid & (dist[d] >= 1) & (dist[d] <= reach(j)))
                def _():
                    scatter(d, j).wait_recv()

                @pl.when(valid & (dist[d] < reach(j)))
                def _():
                    scatter(d, j).start()

    def order():
        loads[2].wait()
        kk = lax.broadcasted_iota(jnp.int32, (NB, NB), 0)
        perm = (kk == (one_ref[...] & (NB - 1))).astype(F32).astype(BF16)
        hi, lo = split(linv[...])
        lhi[...] = dot(hi, perm).astype(BF16)
        llo[...] = dot(lo, perm).astype(BF16)

    def base():
        tgt = two_ref[...] >> BITS
        i = lax.broadcasted_iota(jnp.int32, (1, NB), 1)
        again = (tgt == pltpu.roll(tgt, 1, 1)) & (i > 0)
        tgt = jnp.where(again | (tgt < NB), -1, tgt)
        tgt = pltpu.roll(tgt, (NB - HALF * window(z)) % NB, 1)[:, :WIN]
        for r in range(0, rows, 256):
            qq = lax.broadcasted_iota(jnp.int32, (256, WIN), 0) + r
            hit = (qq + off == tgt).astype(F32)
            hot[pl.ds(r, 256), :] = hit.astype(BF16)
            gone = jnp.max(hit, axis=1, keepdims=True) > 0.0
            top = (lax.broadcasted_iota(jnp.int32, (256, 1), 0) + r < NB) & (z == 0)
            out[pl.ds(r, 256), :] = jnp.where(gone | top, 0.0, mat[pl.ds(r, 256), :])

    def weights(r):
        a = pall[:, :, :, r:r + 256].reshape(NB, 256)
        ahi, alo = split(a)
        acc = dot(ahi, lhi[...], 0) + dot(ahi, llo[...], 0) + dot(alo, lhi[...], 0)
        qq = lax.broadcasted_iota(jnp.int32, (256, NB), 0) + r
        own = (qq == (one_ref[...] & (NB - 1))) & (z == 0)
        acc = acc - own.astype(F32)
        hi, lo = split(acc)
        whi[pl.ds(r, 256), :] = hi
        wlo[pl.ds(r, 256), :] = lo

    def product(k, c):
        qhi, qlo = split(q[k // CH:k // CH + 8, :, c:c + 256].reshape(256, 256))
        a, b = whi[:, k:k + 256], wlo[:, k:k + 256]
        return dot(a, qhi) + dot(a, qlo) + dot(b, qhi)

    def update(c):
        out[:, c:c + 256] -= product(0, c)

    def finish(c):
        i = window(z) + lax.broadcasted_iota(jnp.int32, (WIN, 1), 0) // HALF
        near = jnp.where(i < 16, i, 31 - i)
        came = jnp.where(i < 16, dist[0], dist[1]) <= reach(near)
        thi, tlo = split(jnp.where(came, t[pl.ds(window(z), 16), :, c:c + 256].reshape(WIN, 256), 0.0))
        out[:, c:c + 256] += dot(hot[...], thi) + dot(hot[...], tlo) - product(256, c)

    def check():
        i = lax.broadcasted_iota(jnp.int32, (1, NB), 1)

        def block(v):
            return sum((v >= rows * b).astype(jnp.int32) for b in range(1, NZ))

        away = (block(one_ref[...] >> BITS) - z - i // CH + 2 * NZ + 12) % NZ - 8
        late = i % CH >= HALF
        good = (jnp.abs(away) <= 1) | ((away == -2) & ~late) | ((away == 2) & late)
        tgt = two_ref[...] >> BITS
        dest = block(tgt)
        hops = jnp.where(i < NB // 2, dest, NZ - dest)
        near = jnp.where(i < NB // 2, i, NB - 1 - i) // HALF
        inside = i - HALF * window(dest)
        good &= (tgt < NB) | ((inside >= 0) & (inside < WIN) & ((dest == 0) | (hops <= reach(near))))
        misfit[0] = jnp.max(jnp.where(good, 0, 1))

    stripes = list(range(0, cols, 256))
    later = {1: [order], 2: [base, check]}
    for i in range(3):
        later[3 + i] = [functools.partial(weights, 256 * i)]
    for i, c in enumerate(stripes):
        later[6 + i] = [functools.partial(update, c)]

    for i in range(nx - 1):
        pan_x(i).start()
    loads[0].wait()
    take_rows(0, HALF)
    take_rows(112, HALF)
    home(0, 0).start()
    home(1, 0).start()
    fill(0)
    pass_on(0)
    take_rows(16, CH)
    take_rows(80, CH)
    loads[1].wait()

    home(0, 0).wait_recv()
    contrib[pl.ds(80, HALF), :] += left1[...]
    home(0, 1).start()
    home(1, 0).wait_recv()
    contrib[pl.ds(32, HALF), :] += right1[...]
    home(1, 1).start()
    fill(1)
    pass_on(1)
    take_rows(48, CH)
    fill(2)
    for i in range(nx - 1):
        pan_x(i).wait_recv()
    for i in range(ny - 1):
        pan_y(i).start()

    home(0, 1).wait_recv()
    home(1, 1).wait_recv()
    q[4] = contrib[pl.ds(48, CH), :] + left2[...] + right2[...]
    for k in range(1, KSTEP + 1):
        ring(k)
        pass_on(1 + k)
        fill(2 + k)
        if k == 2:
            for i in range(ny - 1):
                pan_y(i).wait_recv()
            if cpart:
                pan_c().start()
        if k == 3 and cpart:
            pan_c().wait_recv()
        for f in later.pop(k, []):
            f()
    for fs in later.values():
        for f in fs:
            f()
    for step in range(KSTEP + 2, NBLOCKS + 10):
        pass_on(step)
    ring(KSTEP + 1)
    for c in stripes:
        finish(c)

    for d in (0, 1):
        home(d, 0).wait_send()
        home(d, 1).wait_send()
        for k in range(1, KSTEP + 1):
            for u in (0, 1):
                on(functools.partial(senders, d, k, u), lambda: gather(d, k, u).wait_send())

        def sent(j, _):
            @pl.when(dist[d] < reach(j))
            def _():
                scatter(d, j).wait_send()

            return 0

        lax.fori_loop(0, 16, sent, 0)
    for i in range(nx - 1):
        pan_x(i).wait_send()
    for i in range(ny - 1):
        pan_y(i).wait_send()
    if cpart:
        pan_c().wait_send()


def plan(touched, anchor, rows, z):
    idx = jnp.arange(NB, dtype=jnp.int32)
    src, owner = anchor[:NB], anchor[:NB] // rows
    tgt, top = touched[NB:], anchor[NB:]

    def rank(group):
        key = group * NB + idx
        return jnp.sum((key[None, :] < key[:, None]).astype(jnp.int32), axis=1)

    def place(pos, values):
        return jnp.sum(jnp.where(pos[:, None] == idx[None, :], values[:, None], 0), axis=0)

    r, s = rank(owner), rank(tgt)
    here = (r - CH * z + 4 * CH) % NB
    one = place(here, src * NB + idx)
    two = place(s, tgt * NB + jnp.clip(top, 0, NB - 1))
    return one, two


def plain(matrix, panel_t, l_inverse, touched, anchor):
    rows = matrix.shape[0]
    offset = lax.axis_index("prow") * rows
    local = anchor - offset
    owned = (local >= 0) & (local < rows)
    picked = jnp.where(owned[:, None], matrix[jnp.clip(local, 0, rows - 1)], 0.0)

    def ring(axis, init):
        n = lax.axis_size(axis)
        pairs = [(i, (i + 1) % n) for i in range(n)]
        return n, lambda v: lax.ppermute(v, axis, pairs), init

    n, shift, _ = ring("prow", None)

    def add(_, carry):
        part, total = carry
        part = shift(part)
        return part, total + part

    _, moved = lax.fori_loop(0, n - 1, add, (picked, picked))
    m, shift_p, _ = ring("pcol", None)
    me = lax.axis_index("pcol")
    wide = jnp.zeros((m,) + panel_t.shape, panel_t.dtype).at[me].set(panel_t)

    def put(i, carry):
        part, whole = carry
        return shift_p(part), lax.dynamic_update_index_in_dim(whole, part, (me - 1 - i) % m, 0)

    _, wide = lax.fori_loop(0, m - 1, put, (shift_p(panel_t), wide))
    high = functools.partial(jnp.dot, precision=lax.Precision.HIGHEST, preferred_element_type=F32)
    upper = high(l_inverse, moved[:NB])
    target = touched - offset
    target = jnp.where((target >= 0) & (target < rows), target, rows)
    lands = jnp.full((rows,), -1, jnp.int32).at[target].set(jnp.arange(2 * NB, dtype=jnp.int32), mode="drop")
    permuted = jnp.where((lands >= 0)[:, None], moved[jnp.clip(lands, 0, 2 * NB - 1)], matrix)
    return permuted - high(wide.reshape(NB, rows).T, upper)


def fast(shape, matrix, panel_t, l_inverse, one, two):
    rows, cols = matrix.shape
    ny, nx, nc = shape
    vmem, smem = pl.BlockSpec(memory_space=pltpu.VMEM), pl.BlockSpec(memory_space=pltpu.SMEM)
    hbm = pl.BlockSpec(memory_space=pl.ANY)
    npan = max(nx + ny - 1, 1)
    dma = pltpu.SemaphoreType.DMA
    return pl.pallas_call(
        functools.partial(kernel, shape),
        out_shape=(pltpu.VMEM((rows, cols), F32), pltpu.SMEM((1,), jnp.int32)),
        in_specs=[smem, smem, vmem, vmem, hbm, hbm, hbm],
        out_specs=(vmem, smem),
        scratch_shapes=[
            pltpu.VMEM((rows, cols), F32),
            pltpu.VMEM((NB, NB), F32),
            pltpu.VMEM((128, cols), F32),
            pltpu.VMEM((HALF, cols), F32),
            pltpu.VMEM((HALF, cols), F32),
            pltpu.VMEM((CH, cols), F32),
            pltpu.VMEM((CH, cols), F32),
            pltpu.VMEM((NZ, CH, cols), F32),
            pltpu.VMEM((32, HALF, cols), F32),
            pltpu.VMEM((ny * nx, nc, panel_t.shape[0], rows), F32),
            pltpu.VMEM((NB, NB), BF16),
            pltpu.VMEM((NB, NB), BF16),
            pltpu.VMEM((rows, NB), BF16),
            pltpu.VMEM((rows, NB), BF16),
            pltpu.VMEM((rows, WIN), BF16),
            dma((4,)), dma((4,)), dma((4 * KSTEP,)), dma((4 * KSTEP,)),
            dma((2, 16)), dma((2, 16)), dma((npan,)), dma((npan,)), dma((3,)),
        ],
        compiler_params=pltpu.CompilerParams(
            collective_id=0, has_side_effects=True, vmem_limit_bytes=40 * 2**20
        ),
    )(one, two, one.reshape(1, NB), two.reshape(1, NB), matrix, panel_t, l_inverse)


def body(shape, matrix, panel, l_inverse, touched, anchor):
    z = lax.axis_index("prow")
    one, two = plan(touched, anchor, matrix.shape[0], z)
    panel_t = panel.T
    done, misfit = fast(shape, matrix, panel_t, l_inverse, one, two)
    return lax.cond(misfit[0] == 0, lambda: done, lambda: plain(matrix, panel_t, l_inverse, touched, anchor))


def solution(mesh):
    n = mesh.shape["pcol"]
    shape = (4, 4, 2) if n == 32 else (1, 1, n)
    in_specs = (P("prow", "pcol"), P("prow", "pcol"), P(), P(), P())
    return jax.shard_map(
        functools.partial(body, shape), mesh=mesh, in_specs=in_specs, out_specs=P("prow", "pcol"), check_vma=False
    )
```

```python
import functools

import jax
import jax.numpy as jnp
from jax import lax
from jax.experimental import pallas as pl
from jax.experimental.pallas import tpu as pltpu
from jax.sharding import PartitionSpec as P

MESH = pl.DeviceIdType.MESH
NZ = 16
CH = 32
HALF = 16
WIN = 256
NB = NZ * CH
BITS = 9
F32, BF16 = jnp.float32, jnp.bfloat16


def reach(j):
    return (j + 1) // 2 + 2


UPWARDS = [(7, 7)] * 5 + [(8, 8)] * 3 + [(7, 7)] * 8
KSTEP = max(max(a, NZ - 1 - a) for p in UPWARDS for a in p)
BLOCKS = [2] * 8


def window(z):
    return jnp.clip(2 * z - 7, 0, 16)


def split(x):
    hi = x.astype(BF16)
    return hi, (x - hi.astype(F32)).astype(BF16)


def dot(a, b, ca=1):
    return lax.dot_general(a, b, (((ca,), (0,)), ((), ())), preferred_element_type=F32)


def kernel(
    shape, one_smem, two_smem, one_ref, two_ref, mat_hbm, pan, linv_hbm, out, misfit,
    mat, linv, contrib, left1, right1, left2, right2, q, t, pall, phi, plo, lhi, llo, whi, wlo, hot,
    p_send, p_recv, g_send, g_recv, s_send, s_recv, pan_send, pan_recv, load,
):
    ny, nx, nc = shape
    rows, cols = mat.shape
    z = lax.axis_index("prow")
    w = lax.axis_index("pcol")
    core, x, y = w % nc, (w // nc) % nx, w // (nc * nx)
    off = z * rows
    up, down = (z + 1) % NZ, (z + NZ - 1) % NZ
    dist = (z, (NZ - z) % NZ)
    nxt = ({"prow": up}, {"prow": down})

    def pcol(yy, xx, cc):
        return {"pcol": (yy * nx + xx) * nc + cc}

    xpart = [pcol(y, (x + d) % nx, core) for d in range(1, nx)]
    ypart = [pcol((y + d) % ny, x, core) for d in range(1, ny)]
    cpart = [pcol(y, x, 1 - core)] if nc == 2 else []
    partners = list(nxt) + xpart + ypart + cpart
    kd = pan.shape[0]

    loads = [
        pltpu.make_async_copy(mat_hbm, mat, load.at[0]),
        pltpu.make_async_copy(pan, pall.at[y, x, core], load.at[1]),
        pltpu.make_async_copy(linv_hbm, linv, load.at[2]),
    ]
    for c in loads:
        c.start()

    barrier = pltpu.get_barrier_semaphore()
    for dev in partners:
        pl.semaphore_signal(barrier, inc=1, device_id=dev, device_id_type=MESH)
    pl.semaphore_wait(barrier, len(partners))

    def remote(src, dst, ss, rs, dev):
        return pltpu.make_async_remote_copy(
            src_ref=src, dst_ref=dst, send_sem=ss, recv_sem=rs, device_id=dev, device_id_type=MESH
        )

    def on(devices, act):
        if len(devices) == NZ:
            act()
            return
        starts = [i for i in sorted(devices) if (i - 1) % NZ not in devices]
        hit = None
        for i in starts:
            n = 1
            while (i + n) % NZ in devices:
                n += 1
            one = (z + NZ - i) % NZ < n
            hit = one if hit is None else hit | one
        if hit is not None:
            pl.when(hit)(act)

    lanes = ((xpart, ypart), (ypart, xpart))
    parts = (pl.ds(0, kd // 2), pl.ds(kd // 2, kd // 2))

    def panel(half, step):
        part = parts[half]
        copies = []
        for i, dev in enumerate(lanes[half][step]):
            if step == 0:
                src, dst = pan.at[part], pall.at[y, x, core, part]
            elif half == 0:
                src = dst = pall.at[y, :, core, part]
            else:
                src = dst = pall.at[:, x, core, part]
            k = (2 * half + step) * 3 + i
            copies.append(remote(src, dst, pan_send.at[k], pan_recv.at[k], dev))
        return copies

    def sibling():
        return remote(pall.at[:, :, core], pall.at[:, :, core], pan_send.at[12], pan_recv.at[12], cpart[0])

    def home(d, k):
        if k == 0:
            src = contrib.at[pl.ds(112, HALF)] if d == 0 else contrib.at[pl.ds(0, HALF)]
            dst = (left1, right1)[d]
        else:
            src = contrib.at[pl.ds(80, CH)] if d == 0 else contrib.at[pl.ds(16, CH)]
            dst = (left2, right2)[d]
        i = 2 * k + d
        return remote(src, dst, p_send.at[i], p_recv.at[i], nxt[d])

    def gather(d, k, u):
        src, dst = ((5 - k) % NZ, (4 - k) % NZ) if d == 0 else (3 + k, 4 + k)
        part = pl.ds(HALF * u, HALF)
        i = (2 * (k - 1) + d) * 2 + u
        return remote(q.at[src, part], q.at[dst, part], g_send.at[i], g_recv.at[i], nxt[d])

    def senders(d, k, u):
        keep = set()
        for i in range(NZ):
            h = (i - (k - 1)) % NZ if d == 0 else (i + (k - 1)) % NZ
            far = UPWARDS[h][u] if d == 0 else NZ - 1 - UPWARDS[h][u]
            if k <= far:
                keep.add(i)
        return keep

    def ring(k, between=()):
        for u in (0, 1):
            for f in between if u == 1 else ():
                f()
            for d in (0, 1):
                if k > 1:
                    came = {(i + (1 if d == 0 else -1)) % NZ for i in senders(d, k - 1, u)}
                    on(came, lambda: gather(d, k - 1, u).wait_recv())
                if k <= KSTEP:
                    on(senders(d, k, u), lambda: gather(d, k, u).start())

    def take_rows(first, count):
        def one(i, _):
            r = first + i
            li = (one_smem[80 + r] >> BITS) - off
            row = mat[pl.ds(jnp.clip(li, 0, rows - 1), 1), :]
            contrib[pl.ds(r, 1), :] = jnp.where((li >= 0) & (li < rows), row, 0.0)
            return 0

        lax.fori_loop(0, count, one, 0, unroll=8)

    def piece(d, j):
        return j if d == 0 else 31 - j

    def scatter(d, j):
        c = piece(d, j)
        return remote(t.at[c], t.at[c], s_send.at[d, j], s_recv.at[d, j], nxt[d])

    nblocks = len(BLOCKS)
    first_of = [15 - sum(BLOCKS[:b]) for b in range(nblocks)]

    def fill(b):
        if b >= nblocks:
            return

        @pl.when(z == 0)
        def _():
            for d in (0, 1):
                base = HALF * (first_of[b] - BLOCKS[b] + 1 if d == 0 else 31 - first_of[b])

                def one(i, _):
                    r = base + i
                    row = mat[pl.ds(jnp.clip(two_smem[r] & (NB - 1), 0, rows - 1), 1), :]
                    t[r // HALF, pl.ds(r % HALF, 1), :] = row
                    return 0

                lax.fori_loop(0, HALF * BLOCKS[b], one, 0, unroll=8)

    def pass_on(step):
        for d in (0, 1):
            b = step - dist[d]
            first, count = jnp.int32(0), jnp.int32(0)
            for i in range(nblocks):
                first = jnp.where(b == i, first_of[i], first)
                count = jnp.where(b == i, BLOCKS[i], count)
            for u in range(max(BLOCKS)):
                j = jnp.clip(first - u, 0, 15)
                valid = u < count

                @pl.when(valid & (dist[d] >= 1) & (dist[d] <= reach(j)))
                def _():
                    scatter(d, j).wait_recv()

                @pl.when(valid & (dist[d] < reach(j)))
                def _():
                    scatter(d, j).start()

    def order(dst, low):
        kk = lax.broadcasted_iota(jnp.int32, (NB, NB), 0)
        perm = (kk == (one_ref[...] & (NB - 1))).astype(F32).astype(BF16)
        dst[...] = dot(split(linv[...])[low], perm).astype(BF16)

    def base(r):
        tgt = two_ref[...] >> BITS
        i = lax.broadcasted_iota(jnp.int32, (1, NB), 1)
        again = (tgt == pltpu.roll(tgt, 1, 1)) & (i > 0)
        tgt = jnp.where(again | (tgt < NB), -1, tgt)
        tgt = pltpu.roll(tgt, (NB - HALF * window(z)) % NB, 1)[:, :WIN]
        qq = lax.broadcasted_iota(jnp.int32, (256, WIN), 0) + r
        hit = (qq + off == tgt).astype(F32)
        hot[pl.ds(r, 256), :] = hit.astype(BF16)
        gone = jnp.max(hit, axis=1, keepdims=True) > 0.0
        top = (lax.broadcasted_iota(jnp.int32, (256, 1), 0) + r < NB) & (z == 0)
        out[pl.ds(r, 256), :] = jnp.where(gone | top, 0.0, mat[pl.ds(r, 256), :])

    def turn(r):
        hi, lo = split(pall[:, :, :, :, r:r + 256].reshape(NB, 256).T)
        phi[pl.ds(r, 256), :] = hi
        plo[pl.ds(r, 256), :] = lo

    def weights(r):
        ahi, alo = phi[pl.ds(r, 256), :], plo[pl.ds(r, 256), :]
        acc = dot(ahi, lhi[...]) + dot(ahi, llo[...]) + dot(alo, lhi[...])
        qq = lax.broadcasted_iota(jnp.int32, (256, NB), 0) + r
        own = (qq == (one_ref[...] & (NB - 1))) & (z == 0)
        acc = acc - own.astype(F32)
        hi, lo = split(acc)
        whi[pl.ds(r, 256), :] = hi
        wlo[pl.ds(r, 256), :] = lo

    def product(k, c):
        qhi, qlo = split(q[k // CH:k // CH + 8, :, c:c + 256].reshape(256, 256))
        a, b = whi[:, k:k + 256], wlo[:, k:k + 256]
        return dot(a, qhi) + dot(a, qlo) + dot(b, qhi)

    def update(c):
        out[:, c:c + 256] -= product(0, c)

    def finish(c):
        i = window(z) + lax.broadcasted_iota(jnp.int32, (WIN, 1), 0) // HALF
        near = jnp.where(i < 16, i, 31 - i)
        came = jnp.where(i < 16, dist[0], dist[1]) <= reach(near)
        thi, tlo = split(jnp.where(came, t[pl.ds(window(z), 16), :, c:c + 256].reshape(WIN, 256), 0.0))
        out[:, c:c + 256] += dot(hot[...], thi) + dot(hot[...], tlo) - product(256, c)

    def check():
        i = lax.broadcasted_iota(jnp.int32, (1, NB), 1)

        def block(v):
            return sum((v >= rows * b).astype(jnp.int32) for b in range(1, NZ))

        away = (block(one_ref[...] >> BITS) - z - i // CH + 2 * NZ + 12) % NZ - 8
        late = i % CH >= HALF
        good = (jnp.abs(away) <= 1) | ((away == -2) & ~late) | ((away == 2) & late)
        tgt = two_ref[...] >> BITS
        dest = block(tgt)
        hops = jnp.where(i < NB // 2, dest, NZ - dest)
        near = jnp.where(i < NB // 2, i, NB - 1 - i) // HALF
        inside = i - HALF * window(dest)
        good &= (tgt < NB) | ((inside >= 0) & (inside < WIN) & ((dest == 0) | (hops <= reach(near))))
        misfit[0] = jnp.max(jnp.where(good, 0, 1))

    stripes = list(range(0, cols, 256))
    call = functools.partial
    turns, prods, ups = ([call(f, 256 * i) for i in range(3)] for f in (turn, weights, update))
    bases = [call(base, 256 * i) for i in range(3)]
    work = {
        1: ([call(order, llo, 1)], [bases[0]]),
        2: ([bases[1]], [bases[2], check]),
        3: ([], []),
        4: ([], [turns[0]]),
        5: ([turns[1]], [turns[2], prods[0]]),
        6: ([prods[1]], [prods[2]]),
        7: ([ups[0]], [ups[1]]),
        8: ([ups[2]], []),
    }
    if len(stripes) < 3:
        work[7], work[8] = ([ups[0]], []), ([], [])

    for half in (0, 1):
        for c in panel(half, 0):
            c.start()
    loads[0].wait()
    take_rows(0, HALF)
    take_rows(112, HALF)
    home(0, 0).start()
    home(1, 0).start()
    fill(0)
    pass_on(0)
    take_rows(16, CH)
    take_rows(80, CH)
    loads[1].wait()
    for half in (0, 1):
        for c in panel(half, 0):
            c.wait_recv()
        for c in panel(half, 1):
            c.start()

    home(0, 0).wait_recv()
    contrib[pl.ds(80, HALF), :] += left1[...]
    home(0, 1).start()
    home(1, 0).wait_recv()
    contrib[pl.ds(32, HALF), :] += right1[...]
    home(1, 1).start()
    fill(1)
    pass_on(1)
    take_rows(48, CH)
    fill(2)
    loads[2].wait()
    order(lhi, 0)

    home(0, 1).wait_recv()
    home(1, 1).wait_recv()
    q[4] = contrib[pl.ds(48, CH), :] + left2[...] + right2[...]
    for k in range(1, KSTEP + 1):
        between, after = work[k]
        ring(k, between)
        pass_on(1 + k)
        fill(2 + k)
        if k == 3:
            for half in (0, 1):
                for c in panel(half, 1):
                    c.wait_recv()
            if cpart:
                sibling().start()
        if k == 4 and cpart:
            sibling().wait_recv()
        for f in after:
            f()
    for step in range(KSTEP + 2, nblocks + 10):
        pass_on(step)
    ring(KSTEP + 1)
    for c in stripes:
        finish(c)

    for d in (0, 1):
        home(d, 0).wait_send()
        home(d, 1).wait_send()
        for k in range(1, KSTEP + 1):
            for u in (0, 1):
                on(senders(d, k, u), lambda: gather(d, k, u).wait_send())

        def sent(j, _):
            @pl.when(dist[d] < reach(j))
            def _():
                scatter(d, j).wait_send()

            return 0

        lax.fori_loop(0, 16, sent, 0)
    for half in (0, 1):
        for step in (0, 1):
            for c in panel(half, step):
                c.wait_send()
    if cpart:
        sibling().wait_send()


def plan(touched, anchor, rows, z):
    idx = jnp.arange(NB, dtype=jnp.int32)
    src, owner = anchor[:NB], anchor[:NB] // rows
    tgt, top = touched[NB:], anchor[NB:]

    def rank(group):
        key = group * NB + idx
        return jnp.sum((key[None, :] < key[:, None]).astype(jnp.int32), axis=1)

    def place(pos, values):
        return jnp.sum(jnp.where(pos[:, None] == idx[None, :], values[:, None], 0), axis=0)

    r, s = rank(owner), rank(tgt)
    here = (r - CH * z + 4 * CH) % NB
    one = place(here, src * NB + idx)
    two = place(s, tgt * NB + jnp.clip(top, 0, NB - 1))
    return one, two


def plain(matrix, panel_t, l_inverse, touched, anchor):
    rows = matrix.shape[0]
    offset = lax.axis_index("prow") * rows
    local = anchor - offset
    owned = (local >= 0) & (local < rows)
    picked = jnp.where(owned[:, None], matrix[jnp.clip(local, 0, rows - 1)], 0.0)

    def ring(axis, init):
        n = lax.axis_size(axis)
        pairs = [(i, (i + 1) % n) for i in range(n)]
        return n, lambda v: lax.ppermute(v, axis, pairs), init

    n, shift, _ = ring("prow", None)

    def add(_, carry):
        part, total = carry
        part = shift(part)
        return part, total + part

    _, moved = lax.fori_loop(0, n - 1, add, (picked, picked))
    m, shift_p, _ = ring("pcol", None)
    me = lax.axis_index("pcol")
    wide = jnp.zeros((m,) + panel_t.shape, panel_t.dtype).at[me].set(panel_t)

    def put(i, carry):
        part, whole = carry
        return shift_p(part), lax.dynamic_update_index_in_dim(whole, part, (me - 1 - i) % m, 0)

    _, wide = lax.fori_loop(0, m - 1, put, (shift_p(panel_t), wide))
    high = functools.partial(jnp.dot, precision=lax.Precision.HIGHEST, preferred_element_type=F32)
    upper = high(l_inverse, moved[:NB])
    target = touched - offset
    target = jnp.where((target >= 0) & (target < rows), target, rows)
    lands = jnp.full((rows,), -1, jnp.int32).at[target].set(jnp.arange(2 * NB, dtype=jnp.int32), mode="drop")
    permuted = jnp.where((lands >= 0)[:, None], moved[jnp.clip(lands, 0, 2 * NB - 1)], matrix)
    return permuted - high(wide.reshape(NB, rows).T, upper)


def fast(shape, matrix, panel_t, l_inverse, one, two):
    rows, cols = matrix.shape
    ny, nx, nc = shape
    vmem, smem = pl.BlockSpec(memory_space=pltpu.VMEM), pl.BlockSpec(memory_space=pltpu.SMEM)
    hbm = pl.BlockSpec(memory_space=pl.ANY)
    npan = 13
    dma = pltpu.SemaphoreType.DMA
    return pl.pallas_call(
        functools.partial(kernel, shape),
        out_shape=(pltpu.VMEM((rows, cols), F32), pltpu.SMEM((1,), jnp.int32)),
        in_specs=[smem, smem, vmem, vmem, hbm, hbm, hbm],
        out_specs=(vmem, smem),
        scratch_shapes=[
            pltpu.VMEM((rows, cols), F32),
            pltpu.VMEM((NB, NB), F32),
            pltpu.VMEM((128, cols), F32),
            pltpu.VMEM((HALF, cols), F32),
            pltpu.VMEM((HALF, cols), F32),
            pltpu.VMEM((CH, cols), F32),
            pltpu.VMEM((CH, cols), F32),
            pltpu.VMEM((NZ, CH, cols), F32),
            pltpu.VMEM((32, HALF, cols), F32),
            pltpu.VMEM((ny, nx, nc, panel_t.shape[0], rows), F32),
            pltpu.VMEM((rows, NB), BF16),
            pltpu.VMEM((rows, NB), BF16),
            pltpu.VMEM((NB, NB), BF16),
            pltpu.VMEM((NB, NB), BF16),
            pltpu.VMEM((rows, NB), BF16),
            pltpu.VMEM((rows, NB), BF16),
            pltpu.VMEM((rows, WIN), BF16),
            dma((4,)), dma((4,)), dma((4 * KSTEP,)), dma((4 * KSTEP,)),
            dma((2, 16)), dma((2, 16)), dma((npan,)), dma((npan,)), dma((3,)),
        ],
        compiler_params=pltpu.CompilerParams(
            collective_id=0, has_side_effects=True, vmem_limit_bytes=40 * 2**20
        ),
    )(one, two, one.reshape(1, NB), two.reshape(1, NB), matrix, panel_t, l_inverse)


def body(shape, matrix, panel, l_inverse, touched, anchor):
    z = lax.axis_index("prow")
    one, two = plan(touched, anchor, matrix.shape[0], z)
    panel_t = panel.T
    done, misfit = fast(shape, matrix, panel_t, l_inverse, one, two)
    return lax.cond(misfit[0] == 0, lambda: done, lambda: plain(matrix, panel_t, l_inverse, touched, anchor))


def solution(mesh):
    n = mesh.shape["pcol"]
    shape = (4, 4, 2) if n == 32 else (1, 1, n)
    in_specs = (P("prow", "pcol"), P("prow", "pcol"), P(), P(), P())
    return jax.shard_map(
        functools.partial(body, shape), mesh=mesh, in_specs=in_specs, out_specs=P("prow", "pcol"), check_vma=False
    )
```

```python
import functools

import jax
import jax.numpy as jnp
from jax import lax
from jax.experimental import pallas as pl
from jax.experimental.pallas import tpu as pltpu
from jax.sharding import PartitionSpec as P

MESH = pl.DeviceIdType.MESH
NZ = 16
CH = 32
HALF = 16
WIN = 256
NB = NZ * CH
BITS = 9
F32, BF16 = jnp.float32, jnp.bfloat16


def reach(j):
    return (j + 1) // 2 + 2


UPWARDS = [(7, 7)] * 5 + [(8, 8)] * 3 + [(7, 7)] * 8
KSTEP = max(max(a, NZ - 1 - a) for p in UPWARDS for a in p)
BLOCKS = [3, 3, 2, 2, 2, 2, 2]


def window(z):
    return jnp.clip(2 * z - 7, 0, 16)


def split(x):
    hi = x.astype(BF16)
    return hi, (x - hi.astype(F32)).astype(BF16)


def dot(a, b, ca=1):
    return lax.dot_general(a, b, (((ca,), (0,)), ((), ())), preferred_element_type=F32)


def kernel(
    shape, one_smem, two_smem, one_ref, two_ref, mat_hbm, pan, linv_hbm, out, misfit,
    mat, linv, contrib, left1, right1, left2, right2, q, t, pall, phi, plo, lhi, llo, whi, wlo, hot,
    p_send, p_recv, g_send, g_recv, s_send, s_recv, pan_send, pan_recv, load,
):
    ny, nx, nc = shape
    rows, cols = mat.shape
    z = lax.axis_index("prow")
    w = lax.axis_index("pcol")
    core, x, y = w % nc, (w // nc) % nx, w // (nc * nx)
    off = z * rows
    up, down = (z + 1) % NZ, (z + NZ - 1) % NZ
    dist = (z, (NZ - z) % NZ)
    nxt = ({"prow": up}, {"prow": down})
    nxt2 = ({"prow": (z + 2) % NZ}, {"prow": (z + NZ - 2) % NZ})

    def pcol(yy, xx, cc):
        return {"pcol": (yy * nx + xx) * nc + cc}

    xpart = [pcol(y, (x + d) % nx, core) for d in range(1, nx)]
    ypart = [pcol((y + d) % ny, x, core) for d in range(1, ny)]
    cpart = [pcol(y, x, 1 - core)] if nc == 2 else []
    partners = list(nxt) + list(nxt2) + xpart + ypart + cpart
    kd = pan.shape[0]

    loads = [
        pltpu.make_async_copy(mat_hbm, mat, load.at[0]),
        pltpu.make_async_copy(pan, pall.at[y, x, core], load.at[1]),
        pltpu.make_async_copy(linv_hbm, linv, load.at[2]),
    ]
    for c in loads:
        c.start()

    barrier = pltpu.get_barrier_semaphore()
    for dev in partners:
        pl.semaphore_signal(barrier, inc=1, device_id=dev, device_id_type=MESH)
    pl.semaphore_wait(barrier, len(partners))

    def remote(src, dst, ss, rs, dev):
        return pltpu.make_async_remote_copy(
            src_ref=src, dst_ref=dst, send_sem=ss, recv_sem=rs, device_id=dev, device_id_type=MESH
        )

    def on(devices, act):
        if len(devices) == NZ:
            act()
            return
        starts = [i for i in sorted(devices) if (i - 1) % NZ not in devices]
        hit = None
        for i in starts:
            n = 1
            while (i + n) % NZ in devices:
                n += 1
            one = (z + NZ - i) % NZ < n
            hit = one if hit is None else hit | one
        if hit is not None:
            pl.when(hit)(act)

    lanes = ((xpart, ypart), (ypart, xpart))
    parts = (pl.ds(0, kd // 2), pl.ds(kd // 2, kd // 2))

    def panel(half, step):
        part = parts[half]
        copies = []
        for i, dev in enumerate(lanes[half][step]):
            if step == 0:
                src, dst = pan.at[part], pall.at[y, x, core, part]
            elif half == 0:
                src = dst = pall.at[y, :, core, part]
            else:
                src = dst = pall.at[:, x, core, part]
            k = (2 * half + step) * 3 + i
            copies.append(remote(src, dst, pan_send.at[k], pan_recv.at[k], dev))
        return copies

    def sibling():
        return remote(pall.at[:, :, core], pall.at[:, :, core], pan_send.at[12], pan_recv.at[12], cpart[0])

    def home(d, far):
        if far:
            src = contrib.at[pl.ds(112, HALF)] if d == 0 else contrib.at[pl.ds(0, HALF)]
            dst, dev = (left1, right1)[d], nxt2[d]
        else:
            src = contrib.at[pl.ds(80, CH)] if d == 0 else contrib.at[pl.ds(16, CH)]
            dst, dev = (left2, right2)[d], nxt[d]
        i = 2 * far + d
        return remote(src, dst, p_send.at[i], p_recv.at[i], dev)

    def gather(d, k, u):
        src, dst = ((5 - k) % NZ, (4 - k) % NZ) if d == 0 else (3 + k, 4 + k)
        part = pl.ds(HALF * u, HALF)
        i = (2 * (k - 1) + d) * 2 + u
        return remote(q.at[src, part], q.at[dst, part], g_send.at[i], g_recv.at[i], nxt[d])

    def senders(d, k, u):
        keep = set()
        for i in range(NZ):
            h = (i - (k - 1)) % NZ if d == 0 else (i + (k - 1)) % NZ
            far = UPWARDS[h][u] if d == 0 else NZ - 1 - UPWARDS[h][u]
            if k <= far:
                keep.add(i)
        return keep

    def ring(k, between=()):
        for u in (0, 1):
            for f in between if u == 1 else ():
                f()
            for d in (0, 1):
                if k > 1:
                    came = {(i + (1 if d == 0 else -1)) % NZ for i in senders(d, k - 1, u)}
                    on(came, lambda: gather(d, k - 1, u).wait_recv())
                if k <= KSTEP:
                    on(senders(d, k, u), lambda: gather(d, k, u).start())

    def take_rows(first, count):
        def one(i, _):
            r = first + i
            li = (one_smem[80 + r] >> BITS) - off
            row = mat[pl.ds(jnp.clip(li, 0, rows - 1), 1), :]
            contrib[pl.ds(r, 1), :] = jnp.where((li >= 0) & (li < rows), row, 0.0)
            return 0

        lax.fori_loop(0, count, one, 0, unroll=8)

    def piece(d, j):
        return j if d == 0 else 31 - j

    def scatter(d, j):
        c = piece(d, j)
        return remote(t.at[c], t.at[c], s_send.at[d, j], s_recv.at[d, j], nxt[d])

    nblocks = len(BLOCKS)
    first_of = [15 - sum(BLOCKS[:b]) for b in range(nblocks)]

    def fill(b):
        if b >= nblocks:
            return

        @pl.when(z == 0)
        def _():
            for d in (0, 1):
                base = HALF * (first_of[b] - BLOCKS[b] + 1 if d == 0 else 31 - first_of[b])

                def one(i, _):
                    r = base + i
                    row = mat[pl.ds(jnp.clip(two_smem[r] & (NB - 1), 0, rows - 1), 1), :]
                    t[r // HALF, pl.ds(r % HALF, 1), :] = row
                    return 0

                lax.fori_loop(0, HALF * BLOCKS[b], one, 0, unroll=8)

    def pass_on(step):
        for d in (0, 1):
            b = step - dist[d]
            first, count = jnp.int32(0), jnp.int32(0)
            for i in range(nblocks):
                first = jnp.where(b == i, first_of[i], first)
                count = jnp.where(b == i, BLOCKS[i], count)
            for u in range(max(BLOCKS)):
                j = jnp.clip(first - u, 0, 15)
                valid = u < count

                @pl.when(valid & (dist[d] >= 1) & (dist[d] <= reach(j)))
                def _():
                    scatter(d, j).wait_recv()

                @pl.when(valid & (dist[d] < reach(j)))
                def _():
                    scatter(d, j).start()

    def order(dst, low):
        kk = lax.broadcasted_iota(jnp.int32, (NB, NB), 0)
        perm = (kk == (one_ref[...] & (NB - 1))).astype(F32).astype(BF16)
        dst[...] = dot(split(linv[...])[low], perm).astype(BF16)

    def base(r):
        tgt = two_ref[...] >> BITS
        i = lax.broadcasted_iota(jnp.int32, (1, NB), 1)
        again = (tgt == pltpu.roll(tgt, 1, 1)) & (i > 0)
        tgt = jnp.where(again | (tgt < NB), -1, tgt)
        tgt = pltpu.roll(tgt, (NB - HALF * window(z)) % NB, 1)[:, :WIN]
        qq = lax.broadcasted_iota(jnp.int32, (256, WIN), 0) + r
        hit = (qq + off == tgt).astype(F32)
        hot[pl.ds(r, 256), :] = hit.astype(BF16)
        gone = jnp.max(hit, axis=1, keepdims=True) > 0.0
        top = (lax.broadcasted_iota(jnp.int32, (256, 1), 0) + r < NB) & (z == 0)
        out[pl.ds(r, 256), :] = jnp.where(gone | top, 0.0, mat[pl.ds(r, 256), :])

    def turn(r):
        hi, lo = split(pall[:, :, :, :, r:r + 256].reshape(NB, 256).T)
        phi[pl.ds(r, 256), :] = hi
        plo[pl.ds(r, 256), :] = lo

    def weights(r):
        ahi, alo = phi[pl.ds(r, 256), :], plo[pl.ds(r, 256), :]
        acc = dot(ahi, lhi[...]) + dot(ahi, llo[...]) + dot(alo, lhi[...])
        qq = lax.broadcasted_iota(jnp.int32, (256, NB), 0) + r
        own = (qq == (one_ref[...] & (NB - 1))) & (z == 0)
        acc = acc - own.astype(F32)
        hi, lo = split(acc)
        whi[pl.ds(r, 256), :] = hi
        wlo[pl.ds(r, 256), :] = lo

    def product(k, c):
        qhi, qlo = split(q[k // CH:k // CH + 8, :, c:c + 256].reshape(256, 256))
        a, b = whi[:, k:k + 256], wlo[:, k:k + 256]
        return dot(a, qhi) + dot(a, qlo) + dot(b, qhi)

    def update(k, c):
        out[:, c:c + 256] -= product(k, c)

    def finish(c):
        i = window(z) + lax.broadcasted_iota(jnp.int32, (WIN, 1), 0) // HALF
        near = jnp.where(i < 16, i, 31 - i)
        came = jnp.where(i < 16, dist[0], dist[1]) <= reach(near)
        thi, tlo = split(jnp.where(came, t[pl.ds(window(z), 16), :, c:c + 256].reshape(WIN, 256), 0.0))
        out[:, c:c + 256] += dot(hot[...], thi) + dot(hot[...], tlo)

    def check():
        i = lax.broadcasted_iota(jnp.int32, (1, NB), 1)

        def block(v):
            return sum((v >= rows * b).astype(jnp.int32) for b in range(1, NZ))

        away = (block(one_ref[...] >> BITS) - z - i // CH + 2 * NZ + 12) % NZ - 8
        late = i % CH >= HALF
        good = (jnp.abs(away) <= 1) | ((away == -2) & ~late) | ((away == 2) & late)
        tgt = two_ref[...] >> BITS
        dest = block(tgt)
        hops = jnp.where(i < NB // 2, dest, NZ - dest)
        near = jnp.where(i < NB // 2, i, NB - 1 - i) // HALF
        inside = i - HALF * window(dest)
        good &= (tgt < NB) | ((inside >= 0) & (inside < WIN) & ((dest == 0) | (hops <= reach(near))))
        misfit[0] = jnp.max(jnp.where(good, 0, 1))

    stripes = list(range(0, cols, 256))
    call = functools.partial
    turns, prods, ups = ([call(f, 256 * i) for i in range(3)] for f in (turn, weights, call(update, 0)))
    bases = [call(base, 256 * i) for i in range(3)]
    work = {
        1: ([call(order, llo, 1)], [bases[0]]),
        2: ([bases[1]], [bases[2], check]),
        3: ([], []),
        4: ([], [turns[0]]),
        5: ([turns[1]], [turns[2], prods[0]]),
        6: ([prods[1]], [prods[2]]),
        7: ([ups[0]], [ups[1]]),
        8: ([ups[2]], []),
    }
    if len(stripes) < 3:
        work[7], work[8] = ([ups[0]], []), ([], [])

    for half in (0, 1):
        for c in panel(half, 0):
            c.start()
    loads[0].wait()
    take_rows(0, HALF)
    home(1, 1).start()
    take_rows(112, HALF)
    home(0, 1).start()
    take_rows(80, CH)
    home(0, 0).start()
    take_rows(16, CH)
    home(1, 0).start()
    fill(0)
    pass_on(0)
    take_rows(48, CH)
    loads[1].wait()
    loads[2].wait()
    fill(1)
    for half in (0, 1):
        for c in panel(half, 0):
            c.wait_recv()
        for c in panel(half, 1):
            c.start()
    order(lhi, 0)

    for d in (0, 1):
        for far in (0, 1):
            home(d, far).wait_recv()
    q[4, 0:HALF] = (contrib[pl.ds(48, HALF), :] + left1[...]) + (left2[0:HALF] + right2[0:HALF])
    q[4, HALF:CH] = (contrib[pl.ds(64, HALF), :] + right1[...]) + (left2[HALF:CH] + right2[HALF:CH])
    for k in range(1, KSTEP + 1):
        between, after = work[k]
        ring(k, between)
        pass_on(k)
        fill(1 + k)
        if k == 3:
            for half in (0, 1):
                for c in panel(half, 1):
                    c.wait_recv()
            if cpart:
                sibling().start()
        if k == 4 and cpart:
            sibling().wait_recv()
        for f in after:
            f()
    ring(KSTEP + 1)
    for c in stripes:
        update(256, c)
    for step in range(KSTEP + 1, nblocks + 10):
        pass_on(step)
    for c in stripes:
        finish(c)

    for d in (0, 1):
        home(d, 0).wait_send()
        home(d, 1).wait_send()
        for k in range(1, KSTEP + 1):
            for u in (0, 1):
                on(senders(d, k, u), lambda: gather(d, k, u).wait_send())

        def sent(j, _):
            @pl.when(dist[d] < reach(j))
            def _():
                scatter(d, j).wait_send()

            return 0

        lax.fori_loop(0, 16, sent, 0)
    for half in (0, 1):
        for step in (0, 1):
            for c in panel(half, step):
                c.wait_send()
    if cpart:
        sibling().wait_send()


def plan(touched, anchor, rows, z):
    idx = jnp.arange(NB, dtype=jnp.int32)
    src, owner = anchor[:NB], anchor[:NB] // rows
    tgt, top = touched[NB:], anchor[NB:]

    def rank(group):
        key = group * NB + idx
        return jnp.sum((key[None, :] < key[:, None]).astype(jnp.int32), axis=1)

    def place(pos, values):
        return jnp.sum(jnp.where(pos[:, None] == idx[None, :], values[:, None], 0), axis=0)

    r, s = rank(owner), rank(tgt)
    here = (r - CH * z + 4 * CH) % NB
    one = place(here, src * NB + idx)
    two = place(s, tgt * NB + jnp.clip(top, 0, NB - 1))
    return one, two


def plain(matrix, panel_t, l_inverse, touched, anchor):
    rows = matrix.shape[0]
    offset = lax.axis_index("prow") * rows
    local = anchor - offset
    owned = (local >= 0) & (local < rows)
    picked = jnp.where(owned[:, None], matrix[jnp.clip(local, 0, rows - 1)], 0.0)

    def ring(axis, init):
        n = lax.axis_size(axis)
        pairs = [(i, (i + 1) % n) for i in range(n)]
        return n, lambda v: lax.ppermute(v, axis, pairs), init

    n, shift, _ = ring("prow", None)

    def add(_, carry):
        part, total = carry
        part = shift(part)
        return part, total + part

    _, moved = lax.fori_loop(0, n - 1, add, (picked, picked))
    m, shift_p, _ = ring("pcol", None)
    me = lax.axis_index("pcol")
    wide = jnp.zeros((m,) + panel_t.shape, panel_t.dtype).at[me].set(panel_t)

    def put(i, carry):
        part, whole = carry
        return shift_p(part), lax.dynamic_update_index_in_dim(whole, part, (me - 1 - i) % m, 0)

    _, wide = lax.fori_loop(0, m - 1, put, (shift_p(panel_t), wide))
    high = functools.partial(jnp.dot, precision=lax.Precision.HIGHEST, preferred_element_type=F32)
    upper = high(l_inverse, moved[:NB])
    target = touched - offset
    target = jnp.where((target >= 0) & (target < rows), target, rows)
    lands = jnp.full((rows,), -1, jnp.int32).at[target].set(jnp.arange(2 * NB, dtype=jnp.int32), mode="drop")
    permuted = jnp.where((lands >= 0)[:, None], moved[jnp.clip(lands, 0, 2 * NB - 1)], matrix)
    return permuted - high(wide.reshape(NB, rows).T, upper)


def fast(shape, matrix, panel_t, l_inverse, one, two):
    rows, cols = matrix.shape
    ny, nx, nc = shape
    vmem, smem = pl.BlockSpec(memory_space=pltpu.VMEM), pl.BlockSpec(memory_space=pltpu.SMEM)
    hbm = pl.BlockSpec(memory_space=pl.ANY)
    npan = 13
    dma = pltpu.SemaphoreType.DMA
    return pl.pallas_call(
        functools.partial(kernel, shape),
        out_shape=(pltpu.VMEM((rows, cols), F32), pltpu.SMEM((1,), jnp.int32)),
        in_specs=[smem, smem, vmem, vmem, hbm, hbm, hbm],
        out_specs=(vmem, smem),
        scratch_shapes=[
            pltpu.VMEM((rows, cols), F32),
            pltpu.VMEM((NB, NB), F32),
            pltpu.VMEM((128, cols), F32),
            pltpu.VMEM((HALF, cols), F32),
            pltpu.VMEM((HALF, cols), F32),
            pltpu.VMEM((CH, cols), F32),
            pltpu.VMEM((CH, cols), F32),
            pltpu.VMEM((NZ, CH, cols), F32),
            pltpu.VMEM((32, HALF, cols), F32),
            pltpu.VMEM((ny, nx, nc, panel_t.shape[0], rows), F32),
            pltpu.VMEM((rows, NB), BF16),
            pltpu.VMEM((rows, NB), BF16),
            pltpu.VMEM((NB, NB), BF16),
            pltpu.VMEM((NB, NB), BF16),
            pltpu.VMEM((rows, NB), BF16),
            pltpu.VMEM((rows, NB), BF16),
            pltpu.VMEM((rows, WIN), BF16),
            dma((4,)), dma((4,)), dma((4 * KSTEP,)), dma((4 * KSTEP,)),
            dma((2, 16)), dma((2, 16)), dma((npan,)), dma((npan,)), dma((3,)),
        ],
        compiler_params=pltpu.CompilerParams(
            collective_id=0, has_side_effects=True, vmem_limit_bytes=40 * 2**20
        ),
    )(one, two, one.reshape(1, NB), two.reshape(1, NB), matrix, panel_t, l_inverse)


def body(shape, matrix, panel, l_inverse, touched, anchor):
    z = lax.axis_index("prow")
    one, two = plan(touched, anchor, matrix.shape[0], z)
    panel_t = panel.T
    done, misfit = fast(shape, matrix, panel_t, l_inverse, one, two)
    return lax.cond(misfit[0] == 0, lambda: done, lambda: plain(matrix, panel_t, l_inverse, touched, anchor))


def solution(mesh):
    n = mesh.shape["pcol"]
    shape = (4, 4, 2) if n == 32 else (1, 1, n)
    in_specs = (P("prow", "pcol"), P("prow", "pcol"), P(), P(), P())
    return jax.shard_map(
        functools.partial(body, shape), mesh=mesh, in_specs=in_specs, out_specs=P("prow", "pcol"), check_vma=False
    )
```

```python
import functools

import jax
import jax.numpy as jnp
from jax import lax
from jax.experimental import pallas as pl
from jax.experimental.pallas import tpu as pltpu
from jax.sharding import PartitionSpec as P

MESH = pl.DeviceIdType.MESH
NZ = 16
CH = 32
HALF = 16
WIN = 256
NB = NZ * CH
BITS = 9
F32, BF16 = jnp.float32, jnp.bfloat16


def reach(j):
    return (j + 1) // 2 + 2


UPWARDS = (
    [(9, 9), (7, 7), (7, 7), (8, 8), (7, 9), (9, 9), (9, 9), (9, 9),
     (7, 7), (7, 7), (6, 6), (6, 6), (6, 6), (6, 6), (8, 8), (6, 6)],
    [(8, 8), (10, 10), (10, 10), (7, 10), (10, 10), (10, 10), (9, 9), (8, 8),
     (8, 8), (7, 7), (5, 5), (5, 5), (5, 5), (5, 6), (6, 6), (7, 7)],
)
KSTEP = max(max(a, NZ - 1 - a) for table in UPWARDS for p in table for a in p)
BLOCKS = ([2] * 8 + [0], [2, 1, 2, 1, 2, 2, 2, 2, 2])
NBLOCKS = len(BLOCKS[0])
FIRST = tuple([15 - sum(table[:b]) for b in range(NBLOCKS)] for table in BLOCKS)


def window(z):
    return jnp.clip(2 * z - 7, 0, 16)


def split(x):
    hi = x.astype(BF16)
    return hi, (x - hi.astype(F32)).astype(BF16)


def dot(a, b, ca=1):
    return lax.dot_general(a, b, (((ca,), (0,)), ((), ())), preferred_element_type=F32)


def kernel(
    shape, one_smem, two_smem, one_ref, two_ref, mat_hbm, pan, linv_hbm, out, misfit,
    mat, linv, contrib, left1, right1, left2, right2, q, t, pall, phi, plo, lhi, llo, whi, wlo, hot,
    p_send, p_recv, g_send, g_recv, s_send, s_recv, pan_send, pan_recv, load,
):
    ny, nx, nc = shape
    rows, cols = mat.shape
    z = lax.axis_index("prow")
    w = lax.axis_index("pcol")
    core, x, y = w % nc, (w // nc) % nx, w // (nc * nx)
    off = z * rows
    up, down = (z + 1) % NZ, (z + NZ - 1) % NZ
    dist = (z, (NZ - z) % NZ)
    nxt = ({"prow": up}, {"prow": down})
    nxt2 = ({"prow": (z + 2) % NZ}, {"prow": (z + NZ - 2) % NZ})

    def pcol(yy, xx, cc):
        return {"pcol": (yy * nx + xx) * nc + cc}

    xpart = [pcol(y, (x + d) % nx, core) for d in range(1, nx)]
    ypart = [pcol((y + d) % ny, x, core) for d in range(1, ny)]
    cpart = [pcol(y, x, 1 - core)] if nc == 2 else []
    partners = list(nxt) + list(nxt2) + xpart + ypart + cpart
    kd = pan.shape[0]

    loads = [
        pltpu.make_async_copy(mat_hbm, mat, load.at[0]),
        pltpu.make_async_copy(pan, pall.at[y, x, core], load.at[1]),
        pltpu.make_async_copy(linv_hbm, linv, load.at[2]),
    ]
    for c in loads:
        c.start()

    barrier = pltpu.get_barrier_semaphore()
    for dev in partners:
        pl.semaphore_signal(barrier, inc=1, device_id=dev, device_id_type=MESH)
    pl.semaphore_wait(barrier, len(partners))

    def remote(src, dst, ss, rs, dev):
        return pltpu.make_async_remote_copy(
            src_ref=src, dst_ref=dst, send_sem=ss, recv_sem=rs, device_id=dev, device_id_type=MESH
        )

    def among(devices):
        hit = None
        for i in sorted(devices):
            if (i - 1) % NZ in devices:
                continue
            n = 1
            while (i + n) % NZ in devices:
                n += 1
            one = (z + NZ - i) % NZ < n
            hit = one if hit is None else hit | one
        return hit

    def on(devices, act):
        sets = [devices(c) for c in range(nc)]
        if all(len(s) == NZ for s in sets):
            act()
        elif all(s == sets[0] for s in sets):
            if sets[0]:
                pl.when(among(sets[0]))(act)
        else:
            hit = None
            for c, s in enumerate(sets):
                if s:
                    one = core == c if len(s) == NZ else (core == c) & among(s)
                    hit = one if hit is None else hit | one
            pl.when(hit)(act)

    def by_core(table, b):
        return jnp.where(core == 0, table[0][b], table[1][b])

    lanes = ((xpart, ypart), (ypart, xpart))
    parts = (pl.ds(0, kd // 2), pl.ds(kd // 2, kd // 2))

    def panel(half, step):
        part = parts[half]
        copies = []
        for i, dev in enumerate(lanes[half][step]):
            if step == 0:
                src, dst = pan.at[part], pall.at[y, x, core, part]
            elif half == 0:
                src = dst = pall.at[y, :, core, part]
            else:
                src = dst = pall.at[:, x, core, part]
            k = (2 * half + step) * 3 + i
            copies.append(remote(src, dst, pan_send.at[k], pan_recv.at[k], dev))
        return copies

    def sibling():
        return remote(pall.at[:, :, core], pall.at[:, :, core], pan_send.at[12], pan_recv.at[12], cpart[0])

    def home(d, far):
        if far:
            src = contrib.at[pl.ds(112, HALF)] if d == 0 else contrib.at[pl.ds(0, HALF)]
            dst, dev = (left1, right1)[d], nxt2[d]
        else:
            src = contrib.at[pl.ds(80, CH)] if d == 0 else contrib.at[pl.ds(16, CH)]
            dst, dev = (left2, right2)[d], nxt[d]
        i = 2 * far + d
        return remote(src, dst, p_send.at[i], p_recv.at[i], dev)

    def gather(d, k, u):
        src, dst = ((5 - k) % NZ, (4 - k) % NZ) if d == 0 else (3 + k, 4 + k)
        part = pl.ds(HALF * u, HALF)
        i = (2 * (k - 1) + d) * 2 + u
        return remote(q.at[src, part], q.at[dst, part], g_send.at[i], g_recv.at[i], nxt[d])

    def senders(d, k, u, c):
        keep = set()
        for i in range(NZ):
            h = (i - (k - 1)) % NZ if d == 0 else (i + (k - 1)) % NZ
            far = UPWARDS[c][h][u] if d == 0 else NZ - 1 - UPWARDS[c][h][u]
            if k <= far:
                keep.add(i)
        return keep

    def ring(k, between=()):
        for u in (0, 1):
            for f in between if u == 1 else ():
                f()
            for d in (0, 1):
                if k > 1:
                    came = lambda c: {(i + (1 if d == 0 else -1)) % NZ for i in senders(d, k - 1, u, c)}
                    on(came, lambda: gather(d, k - 1, u).wait_recv())
                if k <= KSTEP:
                    on(functools.partial(senders, d, k, u), lambda: gather(d, k, u).start())

    def take_rows(first, count):
        def one(i, _):
            r = first + i
            li = (one_smem[80 + r] >> BITS) - off
            row = mat[pl.ds(jnp.clip(li, 0, rows - 1), 1), :]
            contrib[pl.ds(r, 1), :] = jnp.where((li >= 0) & (li < rows), row, 0.0)
            return 0

        lax.fori_loop(0, count, one, 0, unroll=8)

    def piece(d, j):
        return j if d == 0 else 31 - j

    def scatter(d, j):
        c = piece(d, j)
        return remote(t.at[c], t.at[c], s_send.at[d, j], s_recv.at[d, j], nxt[d])

    def fill(b):
        if b >= NBLOCKS or not any(table[b] for table in BLOCKS):
            return

        @pl.when(z == 0)
        def _():
            def both(v, _):
                c = jnp.where(v % 2 == 0, by_core(FIRST, b) - v // 2, 31 - by_core(FIRST, b) + v // 2)

                def one(i, _):
                    row = mat[pl.ds(jnp.clip(two_smem[c * HALF + i] & (NB - 1), 0, rows - 1), 1), :]
                    t[c, pl.ds(i, 1), :] = row
                    return 0

                return lax.fori_loop(0, HALF, one, 0, unroll=8)

            lax.fori_loop(0, 2 * by_core(BLOCKS, b), both, 0)

    def pass_on(step):
        for d in (0, 1):
            b = step - dist[d]
            first, count = jnp.int32(0), jnp.int32(0)
            for i in range(NBLOCKS):
                first = jnp.where(b == i, by_core(FIRST, i), first)
                count = jnp.where(b == i, by_core(BLOCKS, i), count)
            for u in range(2):
                j = jnp.clip(first - u, 0, 15)
                valid = u < count

                @pl.when(valid & (dist[d] >= 1) & (dist[d] <= reach(j)))
                def _():
                    scatter(d, j).wait_recv()

                @pl.when(valid & (dist[d] < reach(j)))
                def _():
                    scatter(d, j).start()

    def order(dst, low):
        kk = lax.broadcasted_iota(jnp.int32, (NB, NB), 0)
        perm = (kk == (one_ref[...] & (NB - 1))).astype(F32).astype(BF16)
        dst[...] = dot(split(linv[...])[low], perm).astype(BF16)

    def base(r):
        tgt = two_ref[...] >> BITS
        i = lax.broadcasted_iota(jnp.int32, (1, NB), 1)
        again = (tgt == pltpu.roll(tgt, 1, 1)) & (i > 0)
        tgt = jnp.where(again | (tgt < NB), -1, tgt)
        tgt = pltpu.roll(tgt, (NB - HALF * window(z)) % NB, 1)[:, :WIN]
        qq = lax.broadcasted_iota(jnp.int32, (256, WIN), 0) + r
        hit = (qq + off == tgt).astype(F32)
        hot[pl.ds(r, 256), :] = hit.astype(BF16)
        gone = jnp.max(hit, axis=1, keepdims=True) > 0.0
        top = (lax.broadcasted_iota(jnp.int32, (256, 1), 0) + r < NB) & (z == 0)
        out[pl.ds(r, 256), :] = jnp.where(gone | top, 0.0, mat[pl.ds(r, 256), :])

    def turn(r):
        hi, lo = split(pall[:, :, :, :, r:r + 256].reshape(NB, 256).T)
        phi[pl.ds(r, 256), :] = hi
        plo[pl.ds(r, 256), :] = lo

    def weights(r):
        ahi, alo = phi[pl.ds(r, 256), :], plo[pl.ds(r, 256), :]
        acc = dot(ahi, lhi[...]) + dot(ahi, llo[...]) + dot(alo, lhi[...])
        qq = lax.broadcasted_iota(jnp.int32, (256, NB), 0) + r
        own = (qq == (one_ref[...] & (NB - 1))) & (z == 0)
        acc = acc - own.astype(F32)
        hi, lo = split(acc)
        whi[pl.ds(r, 256), :] = hi
        wlo[pl.ds(r, 256), :] = lo

    def product(k, c):
        qhi, qlo = split(q[k // CH:k // CH + 8, :, c:c + 256].reshape(256, 256))
        a, b = whi[:, k:k + 256], wlo[:, k:k + 256]
        return dot(a, qhi) + dot(a, qlo) + dot(b, qhi)

    def update(k, c):
        out[:, c:c + 256] -= product(k, c)

    def finish(c):
        i = window(z) + lax.broadcasted_iota(jnp.int32, (WIN, 1), 0) // HALF
        near = jnp.where(i < 16, i, 31 - i)
        came = jnp.where(i < 16, dist[0], dist[1]) <= reach(near)
        thi, tlo = split(jnp.where(came, t[pl.ds(window(z), 16), :, c:c + 256].reshape(WIN, 256), 0.0))
        out[:, c:c + 256] += dot(hot[...], thi) + dot(hot[...], tlo)

    def check():
        i = lax.broadcasted_iota(jnp.int32, (1, NB), 1)

        def block(v):
            return sum((v >= rows * b).astype(jnp.int32) for b in range(1, NZ))

        away = (block(one_ref[...] >> BITS) - z - i // CH + 2 * NZ + 12) % NZ - 8
        late = i % CH >= HALF
        good = (jnp.abs(away) <= 1) | ((away == -2) & ~late) | ((away == 2) & late)
        tgt = two_ref[...] >> BITS
        dest = block(tgt)
        hops = jnp.where(i < NB // 2, dest, NZ - dest)
        near = jnp.where(i < NB // 2, i, NB - 1 - i) // HALF
        inside = i - HALF * window(dest)
        good &= (tgt < NB) | ((inside >= 0) & (inside < WIN) & ((dest == 0) | (hops <= reach(near))))
        misfit[0] = jnp.max(jnp.where(good, 0, 1))

    stripes = list(range(0, cols, 256))
    call = functools.partial
    turns, prods, ups = ([call(f, 256 * i) for i in range(3)] for f in (turn, weights, call(update, 0)))
    bases = [call(base, 256 * i) for i in range(3)]
    work = {
        1: ([call(order, llo, 1)], [bases[0]]),
        2: ([bases[1]], [bases[2], check]),
        3: ([], []),
        4: ([], [turns[0]]),
        5: ([turns[1]], [turns[2], prods[0]]),
        6: ([prods[1]], [prods[2]]),
        7: ([ups[0]], [ups[1]]),
        8: ([ups[2]], []),
    }
    if len(stripes) < 3:
        work[7], work[8] = ([ups[0]], []), ([], [])

    for half in (0, 1):
        for c in panel(half, 0):
            c.start()
    loads[0].wait()
    take_rows(0, HALF)
    home(1, 1).start()
    take_rows(112, HALF)
    home(0, 1).start()
    take_rows(80, CH)
    home(0, 0).start()
    take_rows(16, CH)
    home(1, 0).start()
    fill(0)
    pass_on(0)
    take_rows(48, CH)
    loads[1].wait()
    loads[2].wait()
    fill(1)
    for half in (0, 1):
        for c in panel(half, 0):
            c.wait_recv()
        for c in panel(half, 1):
            c.start()
    order(lhi, 0)

    for d in (0, 1):
        for far in (0, 1):
            home(d, far).wait_recv()
    q[4, 0:HALF] = (contrib[pl.ds(48, HALF), :] + left1[...]) + (left2[0:HALF] + right2[0:HALF])
    q[4, HALF:CH] = (contrib[pl.ds(64, HALF), :] + right1[...]) + (left2[HALF:CH] + right2[HALF:CH])
    for k in range(1, KSTEP + 1):
        between, after = work.get(k, ([], []))
        ring(k, between)
        pass_on(k)
        fill(1 + k)
        if k == 3:
            for half in (0, 1):
                for c in panel(half, 1):
                    c.wait_recv()
            if cpart:
                sibling().start()
        if k == 4 and cpart:
            sibling().wait_recv()
        for f in after:
            f()
    ring(KSTEP + 1)
    for c in stripes:
        update(256, c)
    for step in range(KSTEP + 1, NBLOCKS + 10):
        pass_on(step)
    for c in stripes:
        finish(c)

    for d in (0, 1):
        home(d, 0).wait_send()
        home(d, 1).wait_send()
        for k in range(1, KSTEP + 1):
            for u in (0, 1):
                on(functools.partial(senders, d, k, u), lambda: gather(d, k, u).wait_send())

        def sent(j, _):
            @pl.when(dist[d] < reach(j))
            def _():
                scatter(d, j).wait_send()

            return 0

        lax.fori_loop(0, 16, sent, 0)
    for half in (0, 1):
        for step in (0, 1):
            for c in panel(half, step):
                c.wait_send()
    if cpart:
        sibling().wait_send()


def plan(touched, anchor, rows, z):
    idx = jnp.arange(NB, dtype=jnp.int32)
    src, owner = anchor[:NB], anchor[:NB] // rows
    tgt, top = touched[NB:], anchor[NB:]

    def rank(group):
        key = group * NB + idx
        return jnp.sum((key[None, :] < key[:, None]).astype(jnp.int32), axis=1)

    def place(pos, values):
        return jnp.sum(jnp.where(pos[:, None] == idx[None, :], values[:, None], 0), axis=0)

    r, s = rank(owner), rank(tgt)
    here = (r - CH * z + 4 * CH) % NB
    one = place(here, src * NB + idx)
    two = place(s, tgt * NB + jnp.clip(top, 0, NB - 1))
    return one, two


def plain(matrix, panel_t, l_inverse, touched, anchor):
    rows = matrix.shape[0]
    offset = lax.axis_index("prow") * rows
    local = anchor - offset
    owned = (local >= 0) & (local < rows)
    picked = jnp.where(owned[:, None], matrix[jnp.clip(local, 0, rows - 1)], 0.0)

    def ring(axis, init):
        n = lax.axis_size(axis)
        pairs = [(i, (i + 1) % n) for i in range(n)]
        return n, lambda v: lax.ppermute(v, axis, pairs), init

    n, shift, _ = ring("prow", None)

    def add(_, carry):
        part, total = carry
        part = shift(part)
        return part, total + part

    _, moved = lax.fori_loop(0, n - 1, add, (picked, picked))
    m, shift_p, _ = ring("pcol", None)
    me = lax.axis_index("pcol")
    wide = jnp.zeros((m,) + panel_t.shape, panel_t.dtype).at[me].set(panel_t)

    def put(i, carry):
        part, whole = carry
        return shift_p(part), lax.dynamic_update_index_in_dim(whole, part, (me - 1 - i) % m, 0)

    _, wide = lax.fori_loop(0, m - 1, put, (shift_p(panel_t), wide))
    high = functools.partial(jnp.dot, precision=lax.Precision.HIGHEST, preferred_element_type=F32)
    upper = high(l_inverse, moved[:NB])
    target = touched - offset
    target = jnp.where((target >= 0) & (target < rows), target, rows)
    lands = jnp.full((rows,), -1, jnp.int32).at[target].set(jnp.arange(2 * NB, dtype=jnp.int32), mode="drop")
    permuted = jnp.where((lands >= 0)[:, None], moved[jnp.clip(lands, 0, 2 * NB - 1)], matrix)
    return permuted - high(wide.reshape(NB, rows).T, upper)


def fast(shape, matrix, panel_t, l_inverse, one, two):
    rows, cols = matrix.shape
    ny, nx, nc = shape
    vmem, smem = pl.BlockSpec(memory_space=pltpu.VMEM), pl.BlockSpec(memory_space=pltpu.SMEM)
    hbm = pl.BlockSpec(memory_space=pl.ANY)
    npan = 13
    dma = pltpu.SemaphoreType.DMA
    return pl.pallas_call(
        functools.partial(kernel, shape),
        out_shape=(pltpu.VMEM((rows, cols), F32), pltpu.SMEM((1,), jnp.int32)),
        in_specs=[smem, smem, vmem, vmem, hbm, hbm, hbm],
        out_specs=(vmem, smem),
        scratch_shapes=[
            pltpu.VMEM((rows, cols), F32),
            pltpu.VMEM((NB, NB), F32),
            pltpu.VMEM((128, cols), F32),
            pltpu.VMEM((HALF, cols), F32),
            pltpu.VMEM((HALF, cols), F32),
            pltpu.VMEM((CH, cols), F32),
            pltpu.VMEM((CH, cols), F32),
            pltpu.VMEM((NZ, CH, cols), F32),
            pltpu.VMEM((32, HALF, cols), F32),
            pltpu.VMEM((ny, nx, nc, panel_t.shape[0], rows), F32),
            pltpu.VMEM((rows, NB), BF16),
            pltpu.VMEM((rows, NB), BF16),
            pltpu.VMEM((NB, NB), BF16),
            pltpu.VMEM((NB, NB), BF16),
            pltpu.VMEM((rows, NB), BF16),
            pltpu.VMEM((rows, NB), BF16),
            pltpu.VMEM((rows, WIN), BF16),
            dma((4,)), dma((4,)), dma((4 * KSTEP,)), dma((4 * KSTEP,)),
            dma((2, 16)), dma((2, 16)), dma((npan,)), dma((npan,)), dma((3,)),
        ],
        compiler_params=pltpu.CompilerParams(
            collective_id=0, has_side_effects=True, vmem_limit_bytes=40 * 2**20
        ),
    )(one, two, one.reshape(1, NB), two.reshape(1, NB), matrix, panel_t, l_inverse)


def body(shape, matrix, panel, l_inverse, touched, anchor):
    z = lax.axis_index("prow")
    one, two = plan(touched, anchor, matrix.shape[0], z)
    panel_t = panel.T
    done, misfit = fast(shape, matrix, panel_t, l_inverse, one, two)
    return lax.cond(misfit[0] == 0, lambda: done, lambda: plain(matrix, panel_t, l_inverse, touched, anchor))


def solution(mesh):
    n = mesh.shape["pcol"]
    shape = (4, 4, 2) if n == 32 else (1, 1, n)
    in_specs = (P("prow", "pcol"), P("prow", "pcol"), P(), P(), P())
    return jax.shard_map(
        functools.partial(body, shape), mesh=mesh, in_specs=in_specs, out_specs=P("prow", "pcol"), check_vma=False
    )
```
